128 devices in a mesh: frames: 32 (over z, x, core), rows: 4 (over y).
Axes of the slice: x: 4, y: 4, z: 4, core: 2. Of those that a mesh axis runs over, the one named last changes fastest.
Arguments:
- latents: bfloat16 [256, 8, 128, 512], P('frames', 'rows'), may hold values from -6 to 6
- gain_one: float32 [512], replicated, may hold values from 0.1 to 1.9
- spatial_weight: bfloat16 [3, 3, 512, 512], replicated, may hold values from -0.09375 to 0.09375
- gain_two: float32 [512], replicated, may hold values from 0.1 to 1.9
- temporal_weight: bfloat16 [3, 512, 512], replicated, may hold values from -0.15625 to 0.15625
- gain_three: float32 [512], replicated, may hold values from 0.1 to 1.9
- query_weight: bfloat16 [512, 512], replicated, as said below
- key_weight: bfloat16 [512, 512], replicated, as said below
- value_weight: bfloat16 [512, 512], replicated, may hold values from -0.25 to 0.25
- out_weight: bfloat16 [512, 512], replicated, may hold values from -0.25 to 0.25
Outputs:
- tokens: bfloat16 [262144, 512], P(('frames', 'rows'))
The draws below stay inside these ranges and needn't reach their ends.
Inputs may be any that keep to these rules, and one draw needn't show every extreme that they name: `query_weight`: a projection matrix with entries of order 512 ** -0.5 or larger. `key_weight`: a projection matrix with entries of order 512 ** -0.5.
All inputs are finite; a program needn't handle non-finite values.
Results may differ from the reference program's by a relative error of at most 0.014.
Values may be sent and summed in bfloat16 or wider, within the bound.
No kernel may reach another device: no remote copies, remote signals or barrier semaphores. Data moves between devices by JAX's collectives and lax.ppermute only.
A program may use at most 128 MiB of HBM per device.

```python
import math
import jax
import jax.numpy as jnp
from jax import lax

C = 512
HEADS = 8
HD = 64
WINDOW = 16
W = 128
FRAMES = 256
HEIGHT = 8


def shared_matrix(key):
    return jax.random.normal(key, (C, C), jnp.float32) * C ** (-0.5)


def draw_key_weight(key, part):
    shared = shared_matrix(key)
    key = jax.random.fold_in(key, 11)
    jitter = jax.random.normal(key, (C, C), jnp.float32) * C ** (-0.5) * 0.3
    return (shared + jitter).astype(jnp.bfloat16)


def draw_query_weight(key, part):
    key = jax.random.fold_in(key, 23)
    independent = jax.random.normal(key, (C, C), jnp.float32) * C ** (-0.5)
    return independent.astype(jnp.bfloat16)


def levels(key, dims, shards, low, top_value):
    def one(axis_at, blocks):
        heights = jax.random.uniform(jax.random.fold_in(jax.random.fold_in(key, 6), axis_at), (blocks,), jnp.float32, low / len(shards), top_value / len(shards))
        return jnp.repeat(jnp.exp(heights), dims[axis_at] // blocks).reshape((-1,) + (1,) * (len(dims) - axis_at - 1))

    factor_of = one(*shards[0])
    for cut in shards[1:]:
        factor_of = factor_of * one(*cut)
    return factor_of


def noise(own_key, dims, width, limit, cuts=(), held_as=jnp.bfloat16):
    loudness = levels(own_key, dims, cuts, -0.22, 0.18) if cuts else 1.0
    entries = jax.random.normal(own_key, dims, jnp.float32) * width * loudness
    return jnp.minimum(jnp.maximum(entries, -limit), limit).astype(held_as)


def setup_inputs(seed: int = 0) -> dict:
    splits = jax.random.split(jax.random.key(seed), 11)
    return {
        "latents": noise(splits[0], (FRAMES, HEIGHT, W, C), 1.0, 6.0, ((0, 32), (1, 4))),
        "gain_one": jnp.clip(1.0 + 0.18 * jax.random.normal(splits[1], (C,), jnp.float32), 0.1, 1.9),
        "spatial_weight": noise(splits[2], (3, 3, C, C), (9 * C) ** -0.5, 0.09375),
        "gain_two": jnp.clip(1.0 + 0.18 * jax.random.normal(splits[3], (C,), jnp.float32), 0.1, 1.9),
        "temporal_weight": noise(splits[4], (3, C, C), (3 * C) ** -0.5, 0.15625),
        "gain_three": jnp.clip(1.0 + 0.18 * jax.random.normal(splits[5], (C,), jnp.float32), 0.1, 1.9),
        "query_weight": draw_query_weight(jax.random.fold_in(splits[10], 71), 0),
        "key_weight": draw_key_weight(jax.random.fold_in(splits[10], 71), 0),
        "value_weight": noise(splits[8], (C, C), C ** -0.5, 0.25),
        "out_weight": noise(splits[9], (C, C), C ** -0.5, 0.25),
    }


def normed(values, gain_row):
    values_f32 = values.astype(jnp.float32)
    mean_square = lax.optimization_barrier(jnp.mean(values_f32 * values_f32, axis=-1, keepdims=True))
    return values_f32 * lax.rsqrt(mean_square + 1e-06) * gain_row

def matmul_rows(left, right):
    shaped = left.reshape(-1, left.shape[-1])
    return jnp.dot(shaped, right, preferred_element_type=jnp.float32).reshape(left.shape[:-1] + (right.shape[-1],))

def reference(latents, gain_one, spatial_weight, gain_two, temporal_weight, gain_three, query_weight, key_weight, value_weight, out_weight):
    normed_one = normed(latents, gain_one).astype(jnp.bfloat16)
    padded = jnp.pad(normed_one, ((0, 0), (1, 1), (1, 1), (0, 0)))
    summed = latents.astype(jnp.float32)
    for row_step in range(3):
        for col_step in range(3):
            window_part = padded[:, row_step:row_step + HEIGHT, col_step:col_step + W, :]
            summed = summed + matmul_rows(window_part, spatial_weight[row_step, col_step])
    mixed_one = summed.astype(jnp.bfloat16)
    gated = jax.nn.silu(normed(mixed_one, gain_two)).astype(jnp.bfloat16)
    gated_padded = jnp.pad(gated, ((2, 0), (0, 0), (0, 0), (0, 0)))
    summed = mixed_one.astype(jnp.float32)
    for kernel_tap in range(3):
        summed = summed + matmul_rows(gated_padded[kernel_tap:kernel_tap + FRAMES], temporal_weight[kernel_tap])
    mixed_two = summed.astype(jnp.bfloat16)
    normed_three = normed(mixed_two, gain_three).astype(jnp.bfloat16).reshape(FRAMES, HEIGHT * W, C)
    queries = matmul_rows(normed_three, query_weight).astype(jnp.bfloat16).reshape(FRAMES, HEIGHT * W, HEADS, HD)
    keys = matmul_rows(normed_three, key_weight).astype(jnp.bfloat16).reshape(FRAMES, HEIGHT * W, HEADS, HD)
    values = matmul_rows(normed_three, value_weight).astype(jnp.bfloat16).reshape(FRAMES, HEIGHT * W, HEADS, HD)
    depth_frames = WINDOW - 1
    keys_padded = jnp.pad(keys, ((depth_frames, 0), (0, 0), (0, 0), (0, 0))).astype(jnp.float32)
    values_padded = jnp.pad(values, ((depth_frames, 0), (0, 0), (0, 0), (0, 0))).astype(jnp.float32)
    queries_f32 = queries.astype(jnp.float32)
    frame_ids = jnp.arange(FRAMES, dtype=jnp.int32)
    score_list = []
    for offset in range(WINDOW):
        shifted = keys_padded[depth_frames - offset:depth_frames - offset + FRAMES]
        score = lax.optimization_barrier(jnp.sum(queries_f32 * shifted, axis=-1)) / math.sqrt(HD)
        allowed = (frame_ids - offset >= 0)[:, None, None]
        score_list.append(jnp.where(allowed, score, jnp.float32(-1e+30)))
    scores = jnp.stack(score_list)
    row_max = lax.optimization_barrier(jnp.max(scores, axis=0, keepdims=True))
    exps = jnp.exp(scores - row_max)
    row_total = lax.optimization_barrier(jnp.sum(exps, axis=0, keepdims=True))
    probs = (exps / row_total).astype(jnp.bfloat16)
    attended = jnp.zeros((FRAMES, HEIGHT * W, HEADS, HD), jnp.float32)
    for offset in range(WINDOW):
        shifted = values_padded[depth_frames - offset:depth_frames - offset + FRAMES]
        attended = attended + probs[offset].astype(jnp.float32)[..., None] * shifted
    attended = attended.astype(jnp.bfloat16).reshape(-1, C)
    result = mixed_two.reshape(-1, C).astype(jnp.float32) + jnp.dot(attended, out_weight, preferred_element_type=jnp.float32)
    return result.astype(jnp.bfloat16)
```

```python
import functools

import jax
import jax.numpy as jnp
from jax import lax
from jax.experimental import pallas as pl
from jax.experimental.pallas import tpu as pltpu
from jax.sharding import PartitionSpec as P

C = 512
HEADS = 8
HD = 64
W = 128
NF = 16
RIM = 16
CUTS = (0, 48, 96, 128)
AXES = ("frames", "rows")
F32 = jnp.float32
BF16 = jnp.bfloat16
ANY = pl.BlockSpec(memory_space=pl.ANY)
SMEM = pl.BlockSpec(memory_space=pltpu.SMEM)
VMEM = pl.BlockSpec(memory_space=pltpu.VMEM)


def routed(x, route):
    frames, rows = lax.axis_size("frames"), lax.axis_size("rows")
    pairs = []
    for f in range(frames):
        for r in range(rows):
            to_f, to_r = route(f, r)
            if 0 <= to_f < frames and 0 <= to_r < rows:
                pairs.append((f * rows + r, to_f * rows + to_r))
    return lax.ppermute(x, AXES, pairs)


def to_sibling(f, r):
    return f ^ 1, r


def to_same_core(f, r):
    return f, (r + 1 if f % 2 == 0 else r - 1)


def to_other_core(f, r):
    return f ^ 1, (r + 1 if f % 2 == 1 else r - 1)


def to_next_chip(f, r):
    return f + 2, r


def rms(v, gain):
    mean_square = jnp.mean(v * v, axis=-1, keepdims=True)
    return v * lax.rsqrt(mean_square + 1e-06) * gain


def mm(a, b):
    return jnp.dot(a, b, preferred_element_type=F32)


def piece_bounds(j):
    lo = 0 if j == 0 else CUTS[j] + RIM
    hi = W if j == len(CUTS) - 2 else CUTS[j + 1] + RIM
    return lo, hi


def conv_kernel(j, n_pieces, *refs):
    core_ref, own, sib = refs[:3]
    same = refs[3 : 3 + n_pieces]
    cross = refs[3 + n_pieces : 3 + 2 * n_pieces]
    g1, g2, w_hbm, mixed, gated, raw, x, wv, row_sems, w_sems = refs[3 + 2 * n_pieces :]
    c0, c1 = CUTS[j], CUTS[j + 1]
    wc = c1 - c0
    lo, hi = max(c0 - RIM, 0), min(c1 + RIM, W)
    wl, off = hi - lo, c0 - lo
    k = core_ref[0]
    copies = []
    for slot, src in enumerate((own, sib)):
        for role, row in ((0, k), (1, 1 - k)):
            copies.append((src.at[:, row, lo:hi, :], raw.at[role, slot * 8 : slot * 8 + 8]))
    first = j + 1 - n_pieces
    for slot, group in enumerate((same, cross)):
        for i in range(n_pieces):
            p0, p1 = piece_bounds(first + i)
            a, b = max(p0, lo), min(p1, hi)
            copies.append(
                (
                    group[i].at[:, a - p0 : b - p0, :],
                    raw.at[2, slot * 8 : slot * 8 + 8, a - lo : b - lo, :],
                )
            )
    row_copies = [
        pltpu.make_async_copy(src, dst, row_sems.at[i]) for i, (src, dst) in enumerate(copies)
    ]
    w_copies = [
        pltpu.make_async_copy(w_hbm.at[tap], wv.at[role], w_sems.at[role])
        for role, tap in enumerate((1, 2 - 2 * k, 2 * k))
    ]
    for copy in row_copies:
        copy.start()
    for copy in w_copies:
        copy.start()
    for copy in row_copies:
        copy.wait()
    gain_one = g1[...]
    gain_two = g2[...]
    row_id = lax.broadcasted_iota(jnp.int32, (wc, C), 0)
    step = max(1, 256 // wc)
    while NF % step:
        step -= 1
    waited = False
    for f0 in range(0, NF, step):
        for role in range(3):
            for f in range(f0, f0 + step):
                v = rms(raw[role, f].astype(F32), gain_one)
                left = pltpu.roll(v, 1, 0)[off : off + wc]
                right = pltpu.roll(v, wl - 1, 0)[off : off + wc]
                if c0 == 0:
                    left = jnp.where(row_id == 0, 0.0, left)
                if c1 == W:
                    right = jnp.where(row_id == wc - 1, 0.0, right)
                rows = slice(f * wc, (f + 1) * wc)
                x[role, rows, 0:C] = left.astype(BF16)
                x[role, rows, C : 2 * C] = v[off : off + wc].astype(BF16)
                x[role, rows, 2 * C : 3 * C] = right.astype(BF16)
        if not waited:
            for copy in w_copies:
                copy.wait()
            waited = True
        rows = slice(f0 * wc, (f0 + step) * wc)
        acc = mm(x[0, rows, :], wv[0]) + mm(x[1, rows, :], wv[1]) + mm(x[2, rows, :], wv[2])
        base = raw[0, f0 : f0 + step, off : off + wc, :].astype(F32)
        one = (acc.reshape(step, wc, C) + base).astype(BF16)
        normed = rms(one.astype(F32), gain_two)
        out = normed / (1.0 + jnp.exp(-normed))
        for i in range(step):
            f = f0 + i
            at = f % 8 + 8 * (k if f < 8 else 1 - k)
            mixed[at] = one[i]
            gated[at] = out[i].astype(BF16)


def conv_stage(j, core, own, sib, same, cross, g1, g2, w):
    c0, c1 = CUTS[j], CUTS[j + 1]
    wc = c1 - c0
    wl = min(c1 + RIM, W) - max(c0 - RIM, 0)
    first = max(0, j - 1)
    same, cross = same[first : j + 1], cross[first : j + 1]
    n = len(same)
    shape = jax.ShapeDtypeStruct((NF, wc, C), BF16)
    return pl.pallas_call(
        functools.partial(conv_kernel, j, n),
        out_shape=(shape, shape),
        in_specs=[SMEM, ANY, ANY] + [ANY] * (2 * n) + [VMEM, VMEM, ANY],
        out_specs=(VMEM, VMEM),
        scratch_shapes=[
            pltpu.VMEM((3, NF, wl, C), BF16),
            pltpu.VMEM((3, NF * wc, 3 * C), BF16),
            pltpu.VMEM((3, 3 * C, C), BF16),
            pltpu.SemaphoreType.DMA((4 + 2 * n,)),
            pltpu.SemaphoreType.DMA((3,)),
        ],
        compiler_params=pltpu.CompilerParams(vmem_limit_bytes=48 * 2**20),
        cost_estimate=pl.CostEstimate(
            flops=2 * NF * wc * 9 * C * C, bytes_accessed=9 * C * C * 2, transcendentals=0
        ),
        name=f"spatial_{j}",
    )(core, own, sib, *same, *cross, g1, g2, w)


def temporal_kernel(wc, gated, before, mixed, w, g3, mixed_two, n_first, n_rest, x):
    x[0 : 2 * wc] = before[...].reshape(2 * wc, C)
    x[2 * wc :] = gated[...].reshape(NF * wc, C)
    gain = g3[...]
    step = max(1, 256 // wc)
    while NF % step:
        step -= 1
    for f0 in range(0, NF, step):
        acc = sum(
            mm(x[(f0 + tap) * wc : (f0 + tap + step) * wc, :], w[tap]) for tap in range(3)
        )
        two = (acc.reshape(step, wc, C) + mixed[f0 : f0 + step].astype(F32)).astype(BF16)
        mixed_two[f0 : f0 + step] = two
        normed = rms(two.astype(F32), gain).astype(BF16)
        for i in range(step):
            if f0 + i == 0:
                n_first[0] = normed[i]
            else:
                n_rest[f0 + i - 1] = normed[i]


def temporal_stage(j, gated, before, mixed, w, g3):
    wc = CUTS[j + 1] - CUTS[j]
    return pl.pallas_call(
        functools.partial(temporal_kernel, wc),
        out_shape=(
            jax.ShapeDtypeStruct((NF, wc, C), BF16),
            jax.ShapeDtypeStruct((1, wc, C), BF16),
            jax.ShapeDtypeStruct((NF - 1, wc, C), BF16),
        ),
        in_specs=[VMEM] * 5,
        out_specs=(VMEM, VMEM, VMEM),
        scratch_shapes=[pltpu.VMEM(((NF + 2) * wc, C), BF16)],
        compiler_params=pltpu.CompilerParams(vmem_limit_bytes=32 * 2**20),
        cost_estimate=pl.CostEstimate(
            flops=2 * NF * wc * 3 * C * C, bytes_accessed=3 * C * C * 2, transcendentals=0
        ),
        name=f"temporal_{j}",
    )(gated, before, mixed, w, g3)


def grouped_store(dst, frame, product, wc):
    for g in range(wc // 8):
        pair = jnp.concatenate(
            [product[g * 8 : g * 8 + 8], product[wc + g * 8 : wc + g * 8 + 8]], axis=0
        )
        dst[g, frame * 8 : frame * 8 + 16, :] = pair.astype(BF16)


def qkv_kernel(wc, n_first, n_rest, wq, wk, wv, q, k, v, x):
    x[0:wc] = n_first[0]
    x[wc:] = n_rest[...].reshape((NF - 1) * wc, C)
    for f0 in range(0, NF, 4):
        rows = x[f0 * wc : (f0 + 4) * wc, :]
        for w, dst, scale in ((wq, q, 0.125), (wk, k, None), (wv, v, None)):
            product = mm(rows, w[...])
            if scale is not None:
                product = product * scale
            grouped_store(dst, f0, product[: 2 * wc], wc)
            grouped_store(dst, f0 + 2, product[2 * wc :], wc)


def qkv_stage(j, n_first, n_rest, wq, wk, wv):
    wc = CUTS[j + 1] - CUTS[j]
    shape = jax.ShapeDtypeStruct((wc // 8, NF * 8, C), BF16)
    return pl.pallas_call(
        functools.partial(qkv_kernel, wc),
        out_shape=(shape,) * 3,
        in_specs=[VMEM] * 5,
        out_specs=(VMEM,) * 3,
        scratch_shapes=[pltpu.VMEM((NF * wc, C), BF16)],
        compiler_params=pltpu.CompilerParams(vmem_limit_bytes=32 * 2**20),
        cost_estimate=pl.CostEstimate(
            flops=2 * NF * wc * 3 * C * C, bytes_accessed=3 * C * C * 2, transcendentals=0
        ),
        name=f"project_{j}",
    )(n_first, n_rest, wq, wk, wv)


def attend_kernel(wc, chip_ref, ctx, wk, wv, wo, q, k, v, mixed_two, out, x, kc, vc, att):
    groups = wc // 8
    rows = NF * 8
    x[0:wc] = jnp.zeros((wc, C), BF16)
    x[wc:] = ctx[...].reshape((NF - 1) * wc, C)
    for f0 in range(0, NF, 4):
        part = x[f0 * wc : (f0 + 4) * wc, :]
        for w, dst in ((wk, kc), (wv, vc)):
            product = mm(part, w[...])
            grouped_store(dst, f0, product[: 2 * wc], wc)
            grouped_store(dst, f0 + 2, product[2 * wc :], wc)
    row = lax.broadcasted_iota(jnp.int32, (rows, 2 * rows), 0)
    key = lax.broadcasted_iota(jnp.int32, (rows, 2 * rows), 1)
    lag = row // 8 + NF - key // 8
    allowed = (row % 8 == key % 8) & (lag >= 0) & (lag < NF)
    allowed = allowed & ((key >= rows) | (chip_ref[0] > 0))
    bias = jnp.where(allowed, 0.0, -1e30).astype(F32)
    lane_head = lax.broadcasted_iota(jnp.int32, (rows, 4 * HD), 1) // HD
    for g in range(groups):
        for half in range(2):
            lanes = slice(half * 4 * HD, (half + 1) * 4 * HD)
            keys = jnp.concatenate([kc[g, :, lanes], k[g, :, lanes]], axis=0)
            values = jnp.concatenate([vc[g, :, lanes], v[g, :, lanes]], axis=0)
            queries = q[g, :, lanes]
            total = jnp.zeros((rows, 4 * HD), F32)
            for h in range(4):
                one = jnp.where(lane_head == h, queries, jnp.zeros_like(queries))
                score = lax.dot_general(
                    one, keys, (((1,), (1,)), ((), ())), preferred_element_type=F32
                )
                score = score + bias
                top = jnp.max(score, axis=-1, keepdims=True)
                e = jnp.exp(score - top)
                scale = 1.0 / jnp.sum(e, axis=-1, keepdims=True)
                got = mm(e.astype(BF16), values) * scale
                total = jnp.where(lane_head == h, got, total)
            att[g, :, lanes] = total.astype(BF16)
    for g in range(0, groups, 2):
        pair = att[g : g + 2].reshape(2 * rows, C)
        product = mm(pair, wo[...])
        for f in range(NF):
            piece = jnp.concatenate(
                [product[f * 8 : f * 8 + 8], product[rows + f * 8 : rows + f * 8 + 8]], axis=0
            )
            cols = slice(g * 8, g * 8 + 16)
            out[f, cols, :] = (piece + mixed_two[f, cols, :].astype(F32)).astype(BF16)


def attend_stage(j, chip, ctx, wk, wv, wo, q, k, v, mixed_two):
    wc = CUTS[j + 1] - CUTS[j]
    groups = wc // 8
    return pl.pallas_call(
        functools.partial(attend_kernel, wc),
        out_shape=jax.ShapeDtypeStruct((NF, wc, C), BF16),
        in_specs=[SMEM] + [VMEM] * 8,
        out_specs=VMEM,
        scratch_shapes=[
            pltpu.VMEM((NF * wc, C), BF16),
            pltpu.VMEM((groups, NF * 8, C), BF16),
            pltpu.VMEM((groups, NF * 8, C), BF16),
            pltpu.VMEM((groups, NF * 8, C), BF16),
        ],
        compiler_params=pltpu.CompilerParams(vmem_limit_bytes=32 * 2**20),
        cost_estimate=pl.CostEstimate(
            flops=2 * NF * wc * 7 * C * C, bytes_accessed=3 * C * C * 2, transcendentals=0
        ),
        name=f"attend_{j}",
    )(chip, ctx, wk, wv, wo, q, k, v, mixed_two)


def shards(
    latents,
    gain_one,
    spatial_weight,
    gain_two,
    temporal_weight,
    gain_three,
    query_weight,
    key_weight,
    value_weight,
    out_weight,
):
    index = lax.axis_index("frames")
    k = index % 2
    core = k.reshape(1).astype(jnp.int32)
    chip = (index // 2).reshape(1).astype(jnp.int32)
    g1, g2, g3 = (g.reshape(1, C) for g in (gain_one, gain_two, gain_three))
    w1 = spatial_weight.reshape(3, 3 * C, C)
    parts = range(len(CUTS) - 1)

    same, cross = [], []
    for j in parts:
        p0, p1 = piece_bounds(j)
        rows = latents[:, :, p0:p1, :]
        outer = lax.dynamic_index_in_dim(rows, 1 - k, 1, keepdims=False)
        inner = lax.dynamic_index_in_dim(rows, k, 1, keepdims=False)
        same.append(routed(outer, to_same_core))
        cross.append(routed(inner, to_other_core))
        if j == 0:
            sib = routed(latents, to_sibling)

    outs = []
    for j in parts:
        mixed_one, gated = conv_stage(j, core, latents, sib, same, cross, g1, g2, w1)
        before = routed(gated[NF - 2 :], to_next_chip)
        mixed_two, n_first, n_rest = temporal_stage(
            j, gated, before, mixed_one, temporal_weight, g3
        )
        ctx = routed(n_rest, to_next_chip)
        q, key, val = qkv_stage(j, n_first, n_rest, query_weight, key_weight, value_weight)
        out = attend_stage(
            j, chip, ctx, key_weight, value_weight, out_weight, q, key, val, mixed_two
        )
        wc = CUTS[j + 1] - CUTS[j]
        chips = lax.axis_size("frames") // 2
        groups = [[c * 8 + i for i in range(8)] for c in range(chips)]
        out = lax.all_to_all(
            out.reshape(8, 2, wc, C), AXES, 0, 0, axis_index_groups=groups
        )
        outs.append(out)
    whole = jnp.concatenate(outs, axis=2)
    whole = whole.reshape(2, 4, 2, W, C).transpose(2, 1, 0, 3, 4)
    return whole.reshape(-1, C)


def solution(mesh):
    placed = (P("frames", "rows", None, None),) + (P(),) * 9
    return jax.shard_map(
        shards, mesh=mesh, in_specs=placed, out_specs=P(("frames", "rows"), None), check_vma=False
    )
```

```python
import functools

import jax
import jax.numpy as jnp
from jax import lax
from jax.experimental import pallas as pl
from jax.experimental.pallas import tpu as pltpu
from jax.sharding import PartitionSpec as P

C = 512
HEADS = 8
HD = 64
W = 128
NF = 16
RIM = 8
EDGE = 2
MAIN = 8 - EDGE
CUTS = (0, 64, 128)
ORDER = ("e0", "i0", "s0", "t0", "i1", "s1", "t1", "p0", "p1", "a0", "w0", "a1", "w1")
AXES = ("frames", "rows")
F32 = jnp.float32
BF16 = jnp.bfloat16
HBM = pl.BlockSpec(memory_space=pltpu.HBM)
SMEM = pl.BlockSpec(memory_space=pltpu.SMEM)
VMEM = pl.BlockSpec(memory_space=pltpu.VMEM)


def routed(x, route):
    frames, rows = lax.axis_size("frames"), lax.axis_size("rows")
    pairs = []
    for f in range(frames):
        for r in range(rows):
            to_f, to_r = route(f, r)
            pairs.append((f * rows + r, to_f % frames * rows + to_r % rows))
    return lax.ppermute(x, AXES, pairs)


def to_sibling(f, r):
    return f ^ 1, r


def to_same_core(f, r):
    return f, (r + 1 if f % 2 == 0 else r - 1)


def to_other_core(f, r):
    return f ^ 1, (r + 1 if f % 2 == 1 else r - 1)


def to_next_chip(f, r):
    return f + 2, r


def pass_on(info, info_out):
    for i in range(4):
        info_out[i] = info[i]


INFO = jax.ShapeDtypeStruct((4,), jnp.int32)


def rms(v, gain):
    mean_square = jnp.mean(v * v, axis=-1, keepdims=True)
    return v * lax.rsqrt(mean_square + 1e-06) * gain


def mm(a, b):
    return jnp.dot(a, b, preferred_element_type=F32)


def piece_bounds(j):
    lo = 0 if j == 0 else CUTS[j] + RIM
    hi = W if j == len(CUTS) - 2 else CUTS[j + 1] + RIM
    return lo, hi


def frames_per_step(count, wc, rows):
    step = max(1, rows // wc)
    while count % step:
        step -= 1
    return step


def window(j):
    c0, c1 = CUTS[j], CUTS[j + 1]
    return c0, c1, max(c0 - 8, 0), min(c1 + 8, W)


def shifted_into(dst, rows, v, bounds):
    c0, c1, lo, hi = bounds
    wc, wl, off = c1 - c0, hi - lo, c0 - lo
    row_id = lax.broadcasted_iota(jnp.int32, (wc, C), 0)
    left = pltpu.roll(v, 1, 0)[off : off + wc]
    right = pltpu.roll(v, wl - 1, 0)[off : off + wc]
    if c0 == 0:
        left = jnp.where(row_id == 0, 0.0, left)
    if c1 == W:
        right = jnp.where(row_id == wc - 1, 0.0, right)
    dst[rows, 0:C] = left.astype(BF16)
    dst[rows, C : 2 * C] = v[off : off + wc].astype(BF16)
    dst[rows, 2 * C : 3 * C] = right.astype(BF16)


def gate_into(mixed, gated, at, total, gain):
    one = total.astype(BF16)
    normed = rms(one.astype(F32), gain)
    mixed[at] = one
    gated[at] = (normed / (1.0 + jnp.exp(-normed))).astype(BF16)


def edge_kernel(info, own, sib, same, cross, g1, g2, w, mixed, gated, info_out, wv, x, sems):
    k = info[0]
    copies = [
        pltpu.make_async_copy(w.at[tap], wv.at[role], sems.at[role])
        for role, tap in enumerate((1, 2 - 2 * k, 2 * k))
    ]
    for copy in copies:
        copy.start()
    pass_on(info, info_out)
    gain = g1[...]
    gain_halo = gain * info[2].astype(F32)
    bounds = (0, W, 0, W)
    for slot in range(2):
        for role in range(3):
            for i in range(EDGE):
                if role < 2:
                    v = (own, sib)[slot][MAIN + i, k if role == 0 else 1 - k]
                else:
                    v = (same, cross)[slot][i]
                v = rms(v.astype(F32), gain_halo if role == 2 else gain)
                shifted_into(x.at[slot, role], slice(i * W, (i + 1) * W), v, bounds)
    for slot in range(2):
        total = (own, sib)[slot][MAIN:8, k].astype(F32).reshape(EDGE * W, C)
        for role in range(3):
            if slot == 0:
                copies[role].wait()
            total = total + mm(x[slot, role], wv[role])
        at = pl.ds(EDGE * (k if slot == 0 else 1 - k), EDGE)
        gate_into(mixed, gated, at, total.reshape(EDGE, W, C), g2[...])


def edge_stage(info, own, sib, same, cross, g1, g2, w):
    shape = jax.ShapeDtypeStruct((2 * EDGE, W, C), BF16)
    return pl.pallas_call(
        edge_kernel,
        out_shape=(shape, shape, INFO, jax.ShapeDtypeStruct((3, 3 * C, C), BF16)),
        in_specs=[SMEM] + [VMEM] * 6 + [HBM],
        out_specs=(VMEM, VMEM, SMEM, VMEM),
        scratch_shapes=[
            pltpu.VMEM((2, 3, EDGE * W, 3 * C), BF16),
            pltpu.SemaphoreType.DMA((3,)),
        ],
        compiler_params=pltpu.CompilerParams(vmem_limit_bytes=24 * 2**20),
        cost_estimate=pl.CostEstimate(
            flops=2 * 4 * W * 9 * C * C, bytes_accessed=9 * C * C * 2, transcendentals=0
        ),
        name="edge",
    )(info, own, sib, same, cross, g1, g2, w)


def inner_kernel(j, info, own, sib, g1, wv, partial, info_out, x):
    pass_on(info, info_out)
    bounds = window(j)
    c0, c1, lo, hi = bounds
    wc = c1 - c0
    k = info[0]
    gain = g1[...]
    step = frames_per_step(MAIN, wc, 256)

    def prepare(index, role):
        for i in range(step):
            slot, at = divmod(index * step + i, MAIN)
            v = (own, sib)[slot][at, k if role == 0 else 1 - k, lo:hi, :].astype(F32)
            shifted_into(x.at[index % 2, role], slice(i * wc, (i + 1) * wc), rms(v, gain), bounds)

    for role in range(2):
        prepare(0, role)
    for index in range(2 * MAIN // step):
        slot, at = divmod(index * step, MAIN)
        acc = (own, sib)[slot][at : at + step, k, c0:c1, :].astype(F32).reshape(step * wc, C)
        for role in range(2):
            acc = acc + mm(x[index % 2, role], wv[role])
            if index + 1 < 2 * MAIN // step:
                prepare(index + 1, role)
        partial[index * step : (index + 1) * step] = acc.reshape(step, wc, C)


def inner_stage(j, info, own, sib, g1, wv):
    c0, c1, _, _ = window(j)
    wc = c1 - c0
    return pl.pallas_call(
        functools.partial(inner_kernel, j),
        out_shape=(jax.ShapeDtypeStruct((2 * MAIN, wc, C), F32), INFO),
        in_specs=[SMEM, VMEM, VMEM, VMEM, VMEM],
        out_specs=(VMEM, SMEM),
        scratch_shapes=[pltpu.VMEM((2, 2, frames_per_step(MAIN, wc, 256) * wc, 3 * C), BF16)],
        compiler_params=pltpu.CompilerParams(vmem_limit_bytes=20 * 2**20),
        cost_estimate=pl.CostEstimate(
            flops=2 * 12 * wc * 6 * C * C, bytes_accessed=6 * C * C * 2, transcendentals=0
        ),
        name=f"inner_{j}",
    )(info, own, sib, g1, wv)


def halo_kernel(j, n_pieces, info, partial, *refs):
    same = refs[:n_pieces]
    cross = refs[n_pieces : 2 * n_pieces]
    g1, g2, wv, mixed, gated, info_out, x = refs[2 * n_pieces :]
    pass_on(info, info_out)
    bounds = window(j)
    c0, c1, lo, hi = bounds
    wc = c1 - c0
    k = info[0]
    first = j + 1 - n_pieces
    gain_one = g1[...] * info[2].astype(F32)
    gain_two = g2[...]
    step = frames_per_step(MAIN, wc, 256)

    def prepare(index):
        for i in range(step):
            slot, at = divmod(index * step + i, MAIN)
            found = []
            for n in range(n_pieces):
                p0, p1 = piece_bounds(first + n)
                begin, end = max(p0, lo), min(p1, hi)
                found.append((same, cross)[slot][n][at, begin - p0 : end - p0, :].astype(F32))
            v = found[0] if n_pieces == 1 else jnp.concatenate(found, axis=0)
            shifted_into(x.at[index % 2], slice(i * wc, (i + 1) * wc), rms(v, gain_one), bounds)

    def finish(index, total):
        slot, at = divmod(index * step, MAIN)
        to = pl.ds(at + MAIN * (k if slot == 0 else 1 - k), step)
        gate_into(mixed, gated, to, total.reshape(step, wc, C), gain_two)

    prepare(0)
    last = None
    for index in range(2 * MAIN // step):
        total = partial[index * step : (index + 1) * step].reshape(step * wc, C)
        total = total + mm(x[index % 2], wv[2])
        if last is not None:
            finish(index - 1, last)
        if index + 1 < 2 * MAIN // step:
            prepare(index + 1)
        last = total
    finish(2 * MAIN // step - 1, last)


def halo_stage(j, info, partial, same, cross, g1, g2, wv):
    c0, c1, _, _ = window(j)
    wc = c1 - c0
    first = max(0, j - 1)
    same, cross = same[first : j + 1], cross[first : j + 1]
    n = len(same)
    shape = jax.ShapeDtypeStruct((2 * MAIN, wc, C), BF16)
    return pl.pallas_call(
        functools.partial(halo_kernel, j, n),
        out_shape=(shape, shape, INFO),
        in_specs=[SMEM] + [VMEM] * (2 * n + 4),
        out_specs=(VMEM, VMEM, SMEM),
        scratch_shapes=[pltpu.VMEM((2, frames_per_step(MAIN, wc, 256) * wc, 3 * C), BF16)],
        compiler_params=pltpu.CompilerParams(vmem_limit_bytes=18 * 2**20),
        cost_estimate=pl.CostEstimate(
            flops=2 * 12 * wc * 3 * C * C, bytes_accessed=3 * C * C * 2, transcendentals=0
        ),
        name=f"halo_{j}",
    )(info, partial, *same, *cross, g1, g2, wv)


def place_of(f):
    core, at = divmod(f, 8)
    return (1, core * EDGE + at - MAIN) if at >= MAIN else (0, core * MAIN + at)


def temporal_kernel(j, info, gated, edge_gated, before, mixed, edge_mixed, w, g3, *refs):
    mixed_two, n_first, n_rest, info_out, x = refs
    pass_on(info, info_out)
    c0, c1 = CUTS[j], CUTS[j + 1]
    wc = c1 - c0
    seen = before[:, c0:c1, :].reshape(2 * wc, C)
    x[0 : 2 * wc] = jnp.where(info[1] > 0, seen, jnp.zeros_like(seen))

    def frame(main, edge, f):
        which, at = place_of(f)
        return edge[at, c0:c1, :] if which else main[at]

    for f in range(NF):
        x[(f + 2) * wc : (f + 3) * wc] = frame(gated, edge_gated, f)
    gain = g3[...]
    step = frames_per_step(NF, wc, 256)
    for f0 in range(0, NF, step):
        acc = sum(
            mm(x[(f0 + tap) * wc : (f0 + tap + step) * wc, :], w[tap]) for tap in range(3)
        )
        for i in range(step):
            f = f0 + i
            base = frame(mixed, edge_mixed, f).astype(F32)
            two = (acc[i * wc : (i + 1) * wc] + base).astype(BF16)
            mixed_two[f] = two
            normed = rms(two.astype(F32), gain).astype(BF16)
            if f == 0:
                n_first[0] = normed
            else:
                n_rest[f - 1] = normed


def temporal_stage(j, info, gated, edge_gated, before, mixed, edge_mixed, w, g3):
    wc = CUTS[j + 1] - CUTS[j]
    return pl.pallas_call(
        functools.partial(temporal_kernel, j),
        out_shape=(
            jax.ShapeDtypeStruct((NF, wc, C), BF16),
            jax.ShapeDtypeStruct((1, wc, C), BF16),
            jax.ShapeDtypeStruct((NF - 1, wc, C), BF16),
            INFO,
        ),
        in_specs=[SMEM] + [VMEM] * 7,
        out_specs=(VMEM, VMEM, VMEM, SMEM),
        scratch_shapes=[pltpu.VMEM(((NF + 2) * wc, C), BF16)],
        compiler_params=pltpu.CompilerParams(vmem_limit_bytes=16 * 2**20),
        cost_estimate=pl.CostEstimate(
            flops=2 * NF * wc * 3 * C * C, bytes_accessed=3 * C * C * 2, transcendentals=0
        ),
        name=f"temporal_{j}",
    )(info, gated, edge_gated, before, mixed, edge_mixed, w, g3)


def grouped_store(dst, frame, product, wc):
    for g in range(wc // 8):
        pair = jnp.concatenate(
            [product[g * 8 : g * 8 + 8], product[wc + g * 8 : wc + g * 8 + 8]], axis=0
        )
        dst[g, frame * 8 : frame * 8 + 16, :] = pair.astype(BF16)


def qkv_kernel(wc, info, n_first, n_rest, wq, wk, wv, q, k, v, info_out, x):
    pass_on(info, info_out)
    x[0:wc] = n_first[0]
    x[wc:] = n_rest[...].reshape((NF - 1) * wc, C)
    for f0 in range(0, NF, 4):
        rows = x[f0 * wc : (f0 + 4) * wc, :]
        for w, dst, scale in ((wq, q, 0.125), (wk, k, None), (wv, v, None)):
            product = mm(rows, w[...])
            if scale is not None:
                product = product * scale
            grouped_store(dst, f0, product[: 2 * wc], wc)
            grouped_store(dst, f0 + 2, product[2 * wc :], wc)


def qkv_stage(j, info, n_first, n_rest, wq, wk, wv):
    wc = CUTS[j + 1] - CUTS[j]
    shape = jax.ShapeDtypeStruct((wc // 8, NF * 8, C), BF16)
    return pl.pallas_call(
        functools.partial(qkv_kernel, wc),
        out_shape=(shape, shape, shape, INFO),
        in_specs=[SMEM] + [VMEM] * 5,
        out_specs=(VMEM, VMEM, VMEM, SMEM),
        scratch_shapes=[pltpu.VMEM((NF * wc, C), BF16)],
        compiler_params=pltpu.CompilerParams(vmem_limit_bytes=20 * 2**20),
        cost_estimate=pl.CostEstimate(
            flops=2 * NF * wc * 3 * C * C, bytes_accessed=3 * C * C * 2, transcendentals=0
        ),
        name=f"project_{j}",
    )(info, n_first, n_rest, wq, wk, wv)


def attend_kernel(wc, info, ctx, wk, wv, wo, q, k, v, mixed_two, *refs):
    blocks, (info_out, x, kc, vc, att, out) = refs[:8], refs[8:]
    pass_on(info, info_out)
    groups = wc // 8
    rows = NF * 8
    x[0:wc] = jnp.zeros((wc, C), BF16)
    x[wc:] = ctx[...].reshape((NF - 1) * wc, C)
    for f0 in range(0, NF, 4):
        part = x[f0 * wc : (f0 + 4) * wc, :]
        for w, dst in ((wk, kc), (wv, vc)):
            product = mm(part, w[...])
            grouped_store(dst, f0, product[: 2 * wc], wc)
            grouped_store(dst, f0 + 2, product[2 * wc :], wc)
    row = lax.broadcasted_iota(jnp.int32, (rows, 2 * rows), 0)
    key = lax.broadcasted_iota(jnp.int32, (rows, 2 * rows), 1)
    lag = row // 8 + NF - key // 8
    allowed = (row % 8 == key % 8) & (lag >= 0) & (lag < NF)
    allowed = allowed & ((key >= rows) | (info[1] > 0))
    bias = jnp.where(allowed, 0.0, -1e30).astype(F32)
    lane_head = lax.broadcasted_iota(jnp.int32, (rows, 4 * HD), 1) // HD
    for g in range(groups):
        for half in range(2):
            lanes = slice(half * 4 * HD, (half + 1) * 4 * HD)
            keys = jnp.concatenate([kc[g, :, lanes], k[g, :, lanes]], axis=0)
            values = jnp.concatenate([vc[g, :, lanes], v[g, :, lanes]], axis=0)
            queries = q[g, :, lanes]
            stacked = jnp.concatenate(
                [jnp.where(lane_head == h, queries, jnp.zeros_like(queries)) for h in range(4)],
                axis=0,
            )
            score = lax.dot_general(
                stacked, keys, (((1,), (1,)), ((), ())), preferred_element_type=F32
            )
            score = score.reshape(4, rows, 2 * rows) + bias[None]
            e = jnp.exp(score - jnp.max(score, axis=-1, keepdims=True))
            scales = 1.0 / jnp.sum(e, axis=-1, keepdims=True)
            got = mm(e.astype(BF16).reshape(4 * rows, 2 * rows), values)
            total, scale = got[:rows], jnp.broadcast_to(scales[0], (rows, 4 * HD))
            for h in range(1, 4):
                total = jnp.where(lane_head == h, got[h * rows : (h + 1) * rows], total)
                scale = jnp.where(lane_head == h, scales[h], scale)
            total = total * scale
            att[g, :, lanes] = total.astype(BF16)
    for g in range(0, groups, 2):
        pair = att[g : g + 2].reshape(2 * rows, C)
        product = mm(pair, wo[...])
        for f in range(NF):
            piece = jnp.concatenate(
                [product[f * 8 : f * 8 + 8], product[rows + f * 8 : rows + f * 8 + 8]], axis=0
            )
            cols = slice(g * 8, g * 8 + 16)
            out[f, cols, :] = (piece + mixed_two[f, cols, :].astype(F32)).astype(BF16)
    core, band = info[0], info[3]
    for n in range(8):
        to_core = core if n < 4 else 1 - core
        blocks[n][...] = out[pl.ds(8 * to_core + 2 * lax.rem(band + n, 4), 2)]


def attend_stage(j, info, ctx, wk, wv, wo, q, k, v, mixed_two):
    wc = CUTS[j + 1] - CUTS[j]
    groups = wc // 8
    return pl.pallas_call(
        functools.partial(attend_kernel, wc),
        out_shape=(jax.ShapeDtypeStruct((2, wc, C), BF16),) * 8 + (INFO,),
        in_specs=[SMEM] + [VMEM] * 8,
        out_specs=(VMEM,) * 8 + (SMEM,),
        scratch_shapes=[
            pltpu.VMEM((NF * wc, C), BF16),
            pltpu.VMEM((groups, NF * 8, C), BF16),
            pltpu.VMEM((groups, NF * 8, C), BF16),
            pltpu.VMEM((groups, NF * 8, C), BF16),
            pltpu.VMEM((NF, wc, C), BF16),
        ],
        compiler_params=pltpu.CompilerParams(vmem_limit_bytes=20 * 2**20),
        cost_estimate=pl.CostEstimate(
            flops=2 * NF * wc * 7 * C * C, bytes_accessed=3 * C * C * 2, transcendentals=0
        ),
        name=f"attend_{j}",
    )(info, ctx, wk, wv, wo, q, k, v, mixed_two)


def place_kernel(j, info, *refs):
    blocks, (out, info_out, sems) = refs[:8], refs[-3:]
    pass_on(info, info_out)
    c0, c1 = CUTS[j], CUTS[j + 1]
    core, band = info[0], info[3]
    copies = []
    for n in range(8):
        from_core = core if n < 4 else 1 - core
        row = 2 * lax.rem(band + 8 - n, 4) + from_core
        copies.append(
            pltpu.make_async_copy(blocks[n], out.at[:, row, c0:c1, :], sems.at[n])
        )
    for copy in copies:
        copy.start()
    for copy in copies:
        copy.wait()


def place_stage(j, info, blocks, whole):
    earlier = () if whole is None else (whole,)
    return pl.pallas_call(
        functools.partial(place_kernel, j),
        out_shape=(jax.ShapeDtypeStruct((2, 8, W, C), BF16), INFO),
        in_specs=[SMEM] + [VMEM] * 8 + [HBM] * len(earlier),
        out_specs=(HBM, SMEM),
        scratch_shapes=[pltpu.SemaphoreType.DMA((8,))],
        input_output_aliases={9: 0} if earlier else {},
        compiler_params=pltpu.CompilerParams(vmem_limit_bytes=8 * 2**20),
        cost_estimate=pl.CostEstimate(flops=0, bytes_accessed=2**21, transcendentals=0),
        name=f"place_{j}",
    )(info, *blocks, *earlier)


def shards(
    latents,
    gain_one,
    spatial_weight,
    gain_two,
    temporal_weight,
    gain_three,
    query_weight,
    key_weight,
    value_weight,
    out_weight,
):
    index = lax.axis_index("frames")
    row = lax.axis_index("rows")
    k = index % 2
    halo_is_inside = jnp.where(k == 0, row > 0, row < lax.axis_size("rows") - 1)
    info = jnp.stack([k, index // 2, halo_is_inside.astype(jnp.int32), row]).astype(jnp.int32)
    g1, g2, g3 = (g.reshape(1, C) for g in (gain_one, gain_two, gain_three))
    w1 = spatial_weight.reshape(3, 3 * C, C)
    parts = range(len(CUTS) - 1)

    def rows_to(frames, columns, which, route, token):
        source = latents if token is None else lax.optimization_barrier((latents, token))[0]
        size = (frames[1] - frames[0], 1, columns[1] - columns[0], C)
        rows = lax.dynamic_slice(source, (frames[0], which, columns[0], 0), size)[:, 0]
        return routed(rows, route), rows

    edge_same, token = rows_to((MAIN, 8), (0, W), 1 - k, to_same_core, None)
    edge_cross, token = rows_to((MAIN, 8), (0, W), k, to_other_core, token)
    sib = routed(latents, to_sibling)
    same, cross = [], []
    for j in parts:
        for group, which, route in ((same, 1 - k, to_same_core), (cross, k, to_other_core)):
            got, token = rows_to((0, MAIN), piece_bounds(j), which, route, token)
            group.append(got)

    state = [{} for _ in parts]
    shared = {}

    def edge(j, info):
        shared["mixed"], shared["gated"], info, shared["w"] = edge_stage(
            info, latents, sib, edge_same, edge_cross, g1, g2, w1
        )
        shared["before"] = routed(shared["gated"][EDGE:], to_next_chip)
        return info

    def inside(j, info):
        state[j]["partial"], info = inner_stage(j, info, latents, sib, g1, shared["w"])
        return info

    def spatial(j, info):
        s = state[j]
        s["mixed"], s["gated"], info = halo_stage(
            j, info, s["partial"], same, cross, g1, g2, shared["w"]
        )
        return info

    def temporal(j, info):
        s = state[j]
        s["mixed"], s["first"], s["rest"], info = temporal_stage(
            j,
            info,
            s["gated"],
            shared["gated"],
            shared["before"],
            s["mixed"],
            shared["mixed"],
            temporal_weight,
            g3,
        )
        s["ctx"] = routed(s["rest"], to_next_chip)
        return info

    def project(j, info):
        s = state[j]
        s["q"], s["k"], s["v"], info = qkv_stage(
            j, info, s["first"], s["rest"], query_weight, key_weight, value_weight
        )
        return info

    def attend(j, info):
        s = state[j]
        *blocks, info = attend_stage(
            j,
            info,
            s["ctx"],
            key_weight,
            value_weight,
            out_weight,
            s["q"],
            s["k"],
            s["v"],
            s["mixed"],
        )
        for n in range(1, 8):
            blocks[n] = routed(blocks[n], lambda f, r: (f ^ (n // 4), r + n))
        s["blocks"] = blocks
        return info

    def place(j, info):
        shared["out"], info = place_stage(j, info, state[j]["blocks"], shared.get("out"))
        return info

    stages = {
        "e": edge,
        "i": inside,
        "s": spatial,
        "t": temporal,
        "p": project,
        "a": attend,
        "w": place,
    }
    for step in ORDER:
        info = stages[step[0]](int(step[1]), info)
    return shared["out"].reshape(-1, C)


def solution(mesh):
    placed = (P("frames", "rows", None, None),) + (P(),) * 9
    return jax.shard_map(
        shards, mesh=mesh, in_specs=placed, out_specs=P(("frames", "rows"), None), check_vma=False
    )
```

```python
import functools

import jax
import jax.numpy as jnp
from jax import lax
from jax.experimental import pallas as pl
from jax.experimental.pallas import tpu as pltpu
from jax.sharding import PartitionSpec as P

C = 512
HEADS = 8
HD = 64
W = 128
NF = 16
RIM = 8
EDGE = 2
MAIN = 8 - EDGE
CUTS = (0, 80, 128)
ORDER = ("e0", "i0", "s0", "t0", "i1", "s1", "t1", "p0", "p1", "a0", "a1", "d0", "d1", "w0", "w1")
AXES = ("frames", "rows")
F32 = jnp.float32
BF16 = jnp.bfloat16
LIGHT = pl.CostEstimate(flops=0, bytes_accessed=0, transcendentals=0)
HBM = pl.BlockSpec(memory_space=pltpu.HBM)
SMEM = pl.BlockSpec(memory_space=pltpu.SMEM)
VMEM = pl.BlockSpec(memory_space=pltpu.VMEM)


def routed(x, route):
    frames, rows = lax.axis_size("frames"), lax.axis_size("rows")
    pairs = []
    for f in range(frames):
        for r in range(rows):
            to_f, to_r = route(f, r)
            pairs.append((f * rows + r, to_f % frames * rows + to_r % rows))
    return lax.ppermute(x, AXES, pairs)


def to_sibling(f, r):
    return f ^ 1, r


def to_same_core(f, r):
    return f, (r + 1 if f % 2 == 0 else r - 1)


def to_other_core(f, r):
    return f ^ 1, (r + 1 if f % 2 == 1 else r - 1)


def to_next_chip(f, r):
    return f + 2, r


def pass_on(info, info_out):
    for i in range(4):
        info_out[i] = info[i]


INFO = jax.ShapeDtypeStruct((4,), jnp.int32)


def rms(v, gain):
    mean_square = jnp.mean(v * v, axis=-1, keepdims=True)
    return v * lax.rsqrt(mean_square + 1e-06) * gain


def mm(a, b):
    return jnp.dot(a, b, preferred_element_type=F32)


def piece_bounds(j):
    lo = 0 if j == 0 else CUTS[j] + RIM
    hi = W if j == len(CUTS) - 2 else CUTS[j + 1] + RIM
    return lo, hi


def frames_per_step(count, wc, rows):
    step = max(1, rows // wc)
    while count % step:
        step -= 1
    return step


def window(j):
    c0, c1 = CUTS[j], CUTS[j + 1]
    return c0, c1, max(c0 - 8, 0), min(c1 + 8, W)


def shifted_into(dst, rows, v, bounds):
    c0, c1, lo, hi = bounds
    wc, wl, off = c1 - c0, hi - lo, c0 - lo
    row_id = lax.broadcasted_iota(jnp.int32, (wc, C), 0)
    left = pltpu.roll(v, 1, 0)[off : off + wc]
    right = pltpu.roll(v, wl - 1, 0)[off : off + wc]
    if c0 == 0:
        left = jnp.where(row_id == 0, 0.0, left)
    if c1 == W:
        right = jnp.where(row_id == wc - 1, 0.0, right)
    dst[rows, 0:C] = left.astype(BF16)
    dst[rows, C : 2 * C] = v[off : off + wc].astype(BF16)
    dst[rows, 2 * C : 3 * C] = right.astype(BF16)


def gate_into(mixed, gated, at, total, gain):
    one = total.astype(BF16)
    normed = rms(one.astype(F32), gain)
    mixed[at] = one
    gated[at] = (normed / (1.0 + jnp.exp(-normed))).astype(BF16)


def first_rows_kernel(info, latents, outer, inner, info_out):
    pass_on(info, info_out)
    k = info[0]
    outer[...] = latents[MAIN:8, 1 - k]
    inner[...] = latents[MAIN:8, k]


def first_rows_stage(info, latents):
    shape = jax.ShapeDtypeStruct((EDGE, W, C), BF16)
    return pl.pallas_call(
        first_rows_kernel,
        out_shape=(shape, shape, INFO),
        in_specs=[SMEM, VMEM],
        out_specs=(VMEM, VMEM, SMEM),
        compiler_params=pltpu.CompilerParams(vmem_limit_bytes=8 * 2**20),
        cost_estimate=LIGHT,
        name="first_rows",
    )(info, latents)


def other_rows_kernel(info, latents, w, *refs):
    *pieces, wv, info_out, sems = refs
    pass_on(info, info_out)
    k = info[0]
    copies = [
        pltpu.make_async_copy(w.at[tap], wv.at[role], sems.at[role])
        for role, tap in enumerate((1, 2 - 2 * k, 2 * k))
    ]
    for copy in copies:
        copy.start()
    for j in range(len(pieces) // 2):
        p0, p1 = piece_bounds(j)
        pieces[2 * j][...] = latents[0:MAIN, 1 - k, p0:p1, :]
        pieces[2 * j + 1][...] = latents[0:MAIN, k, p0:p1, :]
    for copy in copies:
        copy.wait()


def other_rows_stage(info, latents, w):
    shapes = []
    for j in range(len(CUTS) - 1):
        p0, p1 = piece_bounds(j)
        shapes += [jax.ShapeDtypeStruct((MAIN, p1 - p0, C), BF16)] * 2
    shapes.append(jax.ShapeDtypeStruct((3, 3 * C, C), BF16))
    return pl.pallas_call(
        other_rows_kernel,
        out_shape=shapes + [INFO],
        in_specs=[SMEM, VMEM, HBM],
        out_specs=[VMEM] * len(shapes) + [SMEM],
        scratch_shapes=[pltpu.SemaphoreType.DMA((3,))],
        compiler_params=pltpu.CompilerParams(vmem_limit_bytes=16 * 2**20),
        cost_estimate=LIGHT,
        name="other_rows",
    )(info, latents, w)


def edge_kernel(info, own, sib, same, cross, g1, g2, wv, mixed, gated, info_out, x):
    k = info[0]
    pass_on(info, info_out)
    gain = g1[...]
    gain_halo = gain * info[2].astype(F32)
    bounds = (0, W, 0, W)
    for slot in range(2):
        for role in range(3):
            for i in range(EDGE):
                if role < 2:
                    v = (own, sib)[slot][MAIN + i, k if role == 0 else 1 - k]
                else:
                    v = (same, cross)[slot][i]
                v = rms(v.astype(F32), gain_halo if role == 2 else gain)
                shifted_into(x.at[slot, role], slice(i * W, (i + 1) * W), v, bounds)
    for slot in range(2):
        total = (own, sib)[slot][MAIN:8, k].astype(F32).reshape(EDGE * W, C)
        for role in range(3):
            total = total + mm(x[slot, role], wv[role])
        at = pl.ds(EDGE * (k if slot == 0 else 1 - k), EDGE)
        gate_into(mixed, gated, at, total.reshape(EDGE, W, C), g2[...])


def edge_stage(info, own, sib, same, cross, g1, g2, w):
    shape = jax.ShapeDtypeStruct((2 * EDGE, W, C), BF16)
    return pl.pallas_call(
        edge_kernel,
        out_shape=(shape, shape, INFO),
        in_specs=[SMEM] + [VMEM] * 7,
        out_specs=(VMEM, VMEM, SMEM),
        scratch_shapes=[pltpu.VMEM((2, 3, EDGE * W, 3 * C), BF16)],
        compiler_params=pltpu.CompilerParams(vmem_limit_bytes=24 * 2**20),
        cost_estimate=LIGHT,
        name="edge",
    )(info, own, sib, same, cross, g1, g2, w)


def inner_kernel(j, info, own, sib, g1, wv, partial, info_out, x):
    pass_on(info, info_out)
    bounds = window(j)
    c0, c1, lo, hi = bounds
    wc = c1 - c0
    k = info[0]
    gain = g1[...]
    step = frames_per_step(MAIN, wc, 300)

    def prepare(index, role):
        for i in range(step):
            slot, at = divmod(index * step + i, MAIN)
            v = (own, sib)[slot][at, k if role == 0 else 1 - k, lo:hi, :].astype(F32)
            shifted_into(x.at[index % 2, role], slice(i * wc, (i + 1) * wc), rms(v, gain), bounds)

    for role in range(2):
        prepare(0, role)
    for index in range(2 * MAIN // step):
        slot, at = divmod(index * step, MAIN)
        acc = (own, sib)[slot][at : at + step, k, c0:c1, :].astype(F32).reshape(step * wc, C)
        for role in range(2):
            acc = acc + mm(x[index % 2, role], wv[role])
            if index + 1 < 2 * MAIN // step:
                prepare(index + 1, role)
        partial[index * step : (index + 1) * step] = acc.reshape(step, wc, C)


def inner_stage(j, info, own, sib, g1, wv):
    c0, c1, _, _ = window(j)
    wc = c1 - c0
    return pl.pallas_call(
        functools.partial(inner_kernel, j),
        out_shape=(jax.ShapeDtypeStruct((2 * MAIN, wc, C), F32), INFO),
        in_specs=[SMEM, VMEM, VMEM, VMEM, VMEM],
        out_specs=(VMEM, SMEM),
        scratch_shapes=[pltpu.VMEM((2, 2, frames_per_step(MAIN, wc, 300) * wc, 3 * C), BF16)],
        compiler_params=pltpu.CompilerParams(vmem_limit_bytes=20 * 2**20),
        cost_estimate=LIGHT,
        name=f"inner_{j}",
    )(info, own, sib, g1, wv)


def halo_kernel(j, n_pieces, info, partial, *refs):
    same = refs[:n_pieces]
    cross = refs[n_pieces : 2 * n_pieces]
    g1, g2, wv, mixed, gated, info_out, x = refs[2 * n_pieces :]
    pass_on(info, info_out)
    bounds = window(j)
    c0, c1, lo, hi = bounds
    wc = c1 - c0
    k = info[0]
    first = j + 1 - n_pieces
    gain_one = g1[...] * info[2].astype(F32)
    gain_two = g2[...]
    step = frames_per_step(MAIN, wc, 300)

    def prepare(index):
        for i in range(step):
            slot, at = divmod(index * step + i, MAIN)
            found = []
            for n in range(n_pieces):
                p0, p1 = piece_bounds(first + n)
                begin, end = max(p0, lo), min(p1, hi)
                found.append((same, cross)[slot][n][at, begin - p0 : end - p0, :].astype(F32))
            v = found[0] if n_pieces == 1 else jnp.concatenate(found, axis=0)
            shifted_into(x.at[index % 2], slice(i * wc, (i + 1) * wc), rms(v, gain_one), bounds)

    def finish(index, total):
        slot, at = divmod(index * step, MAIN)
        to = pl.ds(at + MAIN * (k if slot == 0 else 1 - k), step)
        gate_into(mixed, gated, to, total.reshape(step, wc, C), gain_two)

    prepare(0)
    last = None
    for index in range(2 * MAIN // step):
        total = partial[index * step : (index + 1) * step].reshape(step * wc, C)
        total = total + mm(x[index % 2], wv[2])
        if last is not None:
            finish(index - 1, last)
        if index + 1 < 2 * MAIN // step:
            prepare(index + 1)
        last = total
    finish(2 * MAIN // step - 1, last)


def halo_stage(j, info, partial, same, cross, g1, g2, wv):
    c0, c1, _, _ = window(j)
    wc = c1 - c0
    first = max(0, j - 1)
    same, cross = same[first : j + 1], cross[first : j + 1]
    n = len(same)
    shape = jax.ShapeDtypeStruct((2 * MAIN, wc, C), BF16)
    return pl.pallas_call(
        functools.partial(halo_kernel, j, n),
        out_shape=(shape, shape, INFO),
        in_specs=[SMEM] + [VMEM] * (2 * n + 4),
        out_specs=(VMEM, VMEM, SMEM),
        scratch_shapes=[pltpu.VMEM((2, frames_per_step(MAIN, wc, 300) * wc, 3 * C), BF16)],
        compiler_params=pltpu.CompilerParams(vmem_limit_bytes=18 * 2**20),
        cost_estimate=LIGHT,
        name=f"halo_{j}",
    )(info, partial, *same, *cross, g1, g2, wv)


def place_of(f):
    core, at = divmod(f, 8)
    return (1, core * EDGE + at - MAIN) if at >= MAIN else (0, core * MAIN + at)


def temporal_kernel(j, info, gated, edge_gated, before, mixed, edge_mixed, w, g3, *refs):
    mixed_two, n_first, n_rest, info_out, x = refs
    pass_on(info, info_out)
    c0, c1 = CUTS[j], CUTS[j + 1]
    wc = c1 - c0
    seen = before[:, c0:c1, :].reshape(2 * wc, C)
    x[0 : 2 * wc] = jnp.where(info[1] > 0, seen, jnp.zeros_like(seen))

    def frame(main, edge, f):
        which, at = place_of(f)
        return edge[at, c0:c1, :] if which else main[at]

    for f in range(NF):
        x[(f + 2) * wc : (f + 3) * wc] = frame(gated, edge_gated, f)
    gain = g3[...]
    step = frames_per_step(NF, wc, 320)
    for f0 in range(0, NF, step):
        acc = sum(
            mm(x[(f0 + tap) * wc : (f0 + tap + step) * wc, :], w[tap]) for tap in range(3)
        )
        for i in range(step):
            f = f0 + i
            base = frame(mixed, edge_mixed, f).astype(F32)
            two = (acc[i * wc : (i + 1) * wc] + base).astype(BF16)
            mixed_two[f] = two
            normed = rms(two.astype(F32), gain).astype(BF16)
            if f == 0:
                n_first[0] = normed
            else:
                n_rest[f - 1] = normed


def temporal_stage(j, info, gated, edge_gated, before, mixed, edge_mixed, w, g3):
    wc = CUTS[j + 1] - CUTS[j]
    return pl.pallas_call(
        functools.partial(temporal_kernel, j),
        out_shape=(
            jax.ShapeDtypeStruct((NF, wc, C), BF16),
            jax.ShapeDtypeStruct((1, wc, C), BF16),
            jax.ShapeDtypeStruct((NF - 1, wc, C), BF16),
            INFO,
        ),
        in_specs=[SMEM] + [VMEM] * 7,
        out_specs=(VMEM, VMEM, VMEM, SMEM),
        scratch_shapes=[pltpu.VMEM(((NF + 2) * wc, C), BF16)],
        compiler_params=pltpu.CompilerParams(vmem_limit_bytes=16 * 2**20),
        cost_estimate=LIGHT,
        name=f"temporal_{j}",
    )(info, gated, edge_gated, before, mixed, edge_mixed, w, g3)


def grouped_store(dst, frame, product, wc):
    for g in range(wc // 8):
        pair = jnp.concatenate(
            [product[g * 8 : g * 8 + 8], product[wc + g * 8 : wc + g * 8 + 8]], axis=0
        )
        dst[g, frame * 8 : frame * 8 + 16, :] = pair.astype(BF16)


def qkv_kernel(wc, info, n_first, n_rest, wq, wk, wv, q, k, v, info_out, x):
    pass_on(info, info_out)
    x[0:wc] = n_first[0]
    x[wc:] = n_rest[...].reshape((NF - 1) * wc, C)
    for f0 in range(0, NF, 4):
        rows = x[f0 * wc : (f0 + 4) * wc, :]
        for w, dst, scale in ((wq, q, 0.125), (wk, k, None), (wv, v, None)):
            product = mm(rows, w[...])
            if scale is not None:
                product = product * scale
            grouped_store(dst, f0, product[: 2 * wc], wc)
            grouped_store(dst, f0 + 2, product[2 * wc :], wc)


def qkv_stage(j, info, n_first, n_rest, wq, wk, wv):
    wc = CUTS[j + 1] - CUTS[j]
    shape = jax.ShapeDtypeStruct((wc // 8, NF * 8, C), BF16)
    return pl.pallas_call(
        functools.partial(qkv_kernel, wc),
        out_shape=(shape, shape, shape, INFO),
        in_specs=[SMEM] + [VMEM] * 5,
        out_specs=(VMEM, VMEM, VMEM, SMEM),
        scratch_shapes=[pltpu.VMEM((NF * wc, C), BF16)],
        compiler_params=pltpu.CompilerParams(vmem_limit_bytes=20 * 2**20),
        cost_estimate=LIGHT,
        name=f"project_{j}",
    )(info, n_first, n_rest, wq, wk, wv)


def attend_kernel(wc, info, ctx, wk, wv, wo, q, k, v, mixed_two, *refs):
    blocks, (info_out, x, kc, vc, att, out) = refs[:4], refs[4:]
    pass_on(info, info_out)
    groups = wc // 8
    rows = NF * 8
    x[0:wc] = jnp.zeros((wc, C), BF16)
    x[wc:] = ctx[...].reshape((NF - 1) * wc, C)
    for f0 in range(0, NF, 4):
        part = x[f0 * wc : (f0 + 4) * wc, :]
        for w, dst in ((wk, kc), (wv, vc)):
            product = mm(part, w[...])
            grouped_store(dst, f0, product[: 2 * wc], wc)
            grouped_store(dst, f0 + 2, product[2 * wc :], wc)
    row = lax.broadcasted_iota(jnp.int32, (rows, 2 * rows), 0)
    key = lax.broadcasted_iota(jnp.int32, (rows, 2 * rows), 1)
    lag = row // 8 + NF - key // 8
    allowed = (row % 8 == key % 8) & (lag >= 0) & (lag < NF)
    allowed = allowed & ((key >= rows) | (info[1] > 0))
    bias = jnp.where(allowed, 0.0, -1e30).astype(F32)
    lane_head = lax.broadcasted_iota(jnp.int32, (rows, 4 * HD), 1) // HD
    for g in range(groups):
        for half in range(2):
            lanes = slice(half * 4 * HD, (half + 1) * 4 * HD)
            keys = jnp.concatenate([kc[g, :, lanes], k[g, :, lanes]], axis=0)
            values = jnp.concatenate([vc[g, :, lanes], v[g, :, lanes]], axis=0)
            queries = q[g, :, lanes]
            stacked = jnp.concatenate(
                [jnp.where(lane_head == h, queries, jnp.zeros_like(queries)) for h in range(4)],
                axis=0,
            )
            score = lax.dot_general(
                stacked, keys, (((1,), (1,)), ((), ())), preferred_element_type=F32
            )
            score = score.reshape(4, rows, 2 * rows) + bias[None]
            e = jnp.exp(score - jnp.max(score, axis=-1, keepdims=True))
            scales = 1.0 / jnp.sum(e, axis=-1, keepdims=True)
            got = mm(e.astype(BF16).reshape(4 * rows, 2 * rows), values)
            total, scale = got[:rows], jnp.broadcast_to(scales[0], (rows, 4 * HD))
            for h in range(1, 4):
                total = jnp.where(lane_head == h, got[h * rows : (h + 1) * rows], total)
                scale = jnp.where(lane_head == h, scales[h], scale)
            total = total * scale
            att[g, :, lanes] = total.astype(BF16)
    for g in range(0, groups, 2):
        pair = att[g : g + 2].reshape(2 * rows, C)
        product = mm(pair, wo[...])
        for f in range(NF):
            piece = jnp.concatenate(
                [product[f * 8 : f * 8 + 8], product[rows + f * 8 : rows + f * 8 + 8]], axis=0
            )
            cols = slice(g * 8, g * 8 + 16)
            out[f, cols, :] = (piece + mixed_two[f, cols, :].astype(F32)).astype(BF16)
    core, band = info[0], info[3]
    for n in range(4):
        at = 2 * lax.rem(band + n, 4)
        blocks[n][0] = out[pl.ds(8 * core + at, 2)]
        blocks[n][1] = out[pl.ds(8 - 8 * core + at, 2)]


def attend_stage(j, info, ctx, wk, wv, wo, q, k, v, mixed_two):
    wc = CUTS[j + 1] - CUTS[j]
    groups = wc // 8
    return pl.pallas_call(
        functools.partial(attend_kernel, wc),
        out_shape=(jax.ShapeDtypeStruct((2, 2, wc, C), BF16),) * 4 + (INFO,),
        in_specs=[SMEM] + [VMEM] * 8,
        out_specs=(VMEM,) * 4 + (SMEM,),
        scratch_shapes=[
            pltpu.VMEM((NF * wc, C), BF16),
            pltpu.VMEM((groups, NF * 8, C), BF16),
            pltpu.VMEM((groups, NF * 8, C), BF16),
            pltpu.VMEM((groups, NF * 8, C), BF16),
            pltpu.VMEM((NF, wc, C), BF16),
        ],
        compiler_params=pltpu.CompilerParams(vmem_limit_bytes=20 * 2**20),
        cost_estimate=LIGHT,
        name=f"attend_{j}",
    )(info, ctx, wk, wv, wo, q, k, v, mixed_two)


def deal_kernel(info, *refs):
    blocks, (give, info_out) = refs[:4], refs[4:]
    pass_on(info, info_out)
    for n in range(4):
        give[n] = blocks[n][1]


def deal_stage(j, info, blocks):
    wc = CUTS[j + 1] - CUTS[j]
    return pl.pallas_call(
        deal_kernel,
        out_shape=(jax.ShapeDtypeStruct((4, 2, wc, C), BF16), INFO),
        in_specs=[SMEM] + [VMEM] * 4,
        out_specs=(VMEM, SMEM),
        compiler_params=pltpu.CompilerParams(vmem_limit_bytes=8 * 2**20),
        cost_estimate=LIGHT,
        name=f"deal_{j}",
    )(info, *blocks)


def place_kernel(j, info, *refs):
    blocks, got, (out, info_out, sems) = refs[:4], refs[4], refs[-3:]
    pass_on(info, info_out)
    c0, c1 = CUTS[j], CUTS[j + 1]
    core, band = info[0], info[3]
    copies = []
    for n in range(4):
        row = 2 * lax.rem(band + 4 - n, 4)
        for i, (src, at) in enumerate(((blocks[n].at[0], core), (got.at[n], 1 - core))):
            dst = out.at[:, row + at, c0:c1, :]
            copies.append(pltpu.make_async_copy(src, dst, sems.at[2 * n + i]))
    for copy in copies:
        copy.start()
    for copy in copies:
        copy.wait()


def place_stage(j, info, blocks, got, whole):
    earlier = () if whole is None else (whole,)
    return pl.pallas_call(
        functools.partial(place_kernel, j),
        out_shape=(jax.ShapeDtypeStruct((2, 8, W, C), BF16), INFO),
        in_specs=[SMEM] + [VMEM] * 5 + [HBM] * len(earlier),
        out_specs=(HBM, SMEM),
        scratch_shapes=[pltpu.SemaphoreType.DMA((8,))],
        input_output_aliases={6: 0} if earlier else {},
        compiler_params=pltpu.CompilerParams(vmem_limit_bytes=8 * 2**20),
        cost_estimate=LIGHT,
        name=f"place_{j}",
    )(info, *blocks, got, *earlier)


def shards(
    latents,
    gain_one,
    spatial_weight,
    gain_two,
    temporal_weight,
    gain_three,
    query_weight,
    key_weight,
    value_weight,
    out_weight,
):
    index = lax.axis_index("frames")
    row = lax.axis_index("rows")
    k = index % 2
    halo_is_inside = jnp.where(k == 0, row > 0, row < lax.axis_size("rows") - 1)
    info = jnp.stack([k, index // 2, halo_is_inside.astype(jnp.int32), row]).astype(jnp.int32)
    g1, g2, g3 = (g.reshape(1, C) for g in (gain_one, gain_two, gain_three))
    w1 = spatial_weight.reshape(3, 3 * C, C)
    parts = range(len(CUTS) - 1)

    sib = routed(latents, to_sibling)
    outer, inner, info = first_rows_stage(info, latents)
    edge_same, edge_cross = routed(outer, to_same_core), routed(inner, to_other_core)
    *pieces, weights, info = other_rows_stage(info, latents, w1)
    *pieces, edge_same, edge_cross = lax.optimization_barrier((*pieces, edge_same, edge_cross))
    own = latents
    same = [routed(piece, to_same_core) for piece in pieces[0::2]]
    cross = [routed(piece, to_other_core) for piece in pieces[1::2]]

    state = [{} for _ in parts]
    shared = {}

    def edge(j, info):
        shared["mixed"], shared["gated"], info = edge_stage(
            info, own, sib, edge_same, edge_cross, g1, g2, weights
        )
        shared["before"] = routed(shared["gated"][EDGE:], to_next_chip)
        return info

    def inside(j, info):
        state[j]["partial"], info = inner_stage(j, info, own, sib, g1, weights)
        return info

    def spatial(j, info):
        s = state[j]
        s["mixed"], s["gated"], info = halo_stage(
            j, info, s["partial"], same, cross, g1, g2, weights
        )
        return info

    def temporal(j, info):
        s = state[j]
        s["mixed"], s["first"], s["rest"], info = temporal_stage(
            j,
            info,
            s["gated"],
            shared["gated"],
            shared["before"],
            s["mixed"],
            shared["mixed"],
            temporal_weight,
            g3,
        )
        s["ctx"] = routed(s["rest"], to_next_chip)
        return info

    def project(j, info):
        s = state[j]
        s["q"], s["k"], s["v"], info = qkv_stage(
            j, info, s["first"], s["rest"], query_weight, key_weight, value_weight
        )
        return info

    def attend(j, info):
        s = state[j]
        *blocks, info = attend_stage(
            j,
            info,
            s["ctx"],
            key_weight,
            value_weight,
            out_weight,
            s["q"],
            s["k"],
            s["v"],
            s["mixed"],
        )
        for n in (2, 1, 3):
            blocks[n] = routed(blocks[n], lambda f, r: (f, r + n))
        s["blocks"] = blocks
        return info

    def deal(j, info):
        s = state[j]
        give, info = deal_stage(j, info, s["blocks"])
        if j + 1 < len(state):
            later = state[j + 1]["blocks"]
            give, *later[1:] = lax.optimization_barrier((give, *later[1:]))
        s["got"] = routed(give, to_sibling)
        return info

    def place(j, info):
        s = state[j]
        shared["out"], info = place_stage(j, info, s["blocks"], s["got"], shared.get("out"))
        return info

    stages = {
        "e": edge,
        "i": inside,
        "s": spatial,
        "t": temporal,
        "p": project,
        "a": attend,
        "d": deal,
        "w": place,
    }
    for step in ORDER:
        info = stages[step[0]](int(step[1]), info)
    return shared["out"].reshape(-1, C)


def solution(mesh):
    placed = (P("frames", "rows", None, None),) + (P(),) * 9
    return jax.shard_map(
        shards, mesh=mesh, in_specs=placed, out_specs=P(("frames", "rows"), None), check_vma=False
    )
```

```python
import functools

import jax
import jax.numpy as jnp
from jax import lax
from jax.experimental import pallas as pl
from jax.experimental.pallas import tpu as pltpu
from jax.sharding import PartitionSpec as P

C = 512
HEADS = 8
HD = 64
W = 128
NF = 16
RIM = 8
EDGE = 2
MAIN = 8 - EDGE
CUTS = (0, 64, 128)
RING = 16
ORDER = ("e0", "i0", "s0", "t0", "i1", "s1", "t1", "p0", "p1", "a0", "a1", "d0", "d1", "w0", "w1")
AXES = ("frames", "rows")
F32 = jnp.float32
BF16 = jnp.bfloat16
LIGHT = pl.CostEstimate(flops=0, bytes_accessed=0, transcendentals=0)
HBM = pl.BlockSpec(memory_space=pltpu.HBM)
SMEM = pl.BlockSpec(memory_space=pltpu.SMEM)
VMEM = pl.BlockSpec(memory_space=pltpu.VMEM)


def routed(x, route):
    frames, rows = lax.axis_size("frames"), lax.axis_size("rows")
    pairs = []
    for f in range(frames):
        for r in range(rows):
            to_f, to_r = route(f, r)
            pairs.append((f * rows + r, to_f % frames * rows + to_r % rows))
    return lax.ppermute(x, AXES, pairs)


def to_sibling(f, r):
    return f ^ 1, r


def to_same_core(f, r):
    return f, (r + 1 if f % 2 == 0 else r - 1)


def to_other_core(f, r):
    return f ^ 1, (r + 1 if f % 2 == 1 else r - 1)


def to_next_chip(f, r):
    return f + 2, r


def pass_on(info, info_out):
    for i in range(4):
        info_out[i] = info[i]


INFO = jax.ShapeDtypeStruct((4,), jnp.int32)


def to_chip_before(f, r):
    core, x = f % 2, f // 2 % 4
    return f // 8 * 8 + (x - 1) % 4 * 2 + core, r


def to_chip_before_last(f, r):
    to_f, _ = to_chip_before(f, r)
    return (to_f + 8 if f // 2 % 4 == 1 else to_f), r


def rms(v, gain):
    mean_square = jnp.mean(v * v, axis=-1, keepdims=True)
    return v * lax.rsqrt(mean_square + 1e-06) * gain


def mm(a, b):
    return jnp.dot(a, b, preferred_element_type=F32)


def piece_bounds(j):
    lo = 0 if j == 0 else CUTS[j] + RIM
    hi = W if j == len(CUTS) - 2 else CUTS[j + 1] + RIM
    return lo, hi


def frames_per_step(count, wc, rows):
    step = max(1, rows // wc)
    while count % step:
        step -= 1
    return step


def window(j):
    c0, c1 = CUTS[j], CUTS[j + 1]
    return c0, c1, max(c0 - 8, 0), min(c1 + 8, W)


def shifted_into(dst, rows, v, bounds):
    c0, c1, lo, hi = bounds
    wc, wl, off = c1 - c0, hi - lo, c0 - lo
    row_id = lax.broadcasted_iota(jnp.int32, (wc, C), 0)
    left = pltpu.roll(v, 1, 0)[off : off + wc]
    right = pltpu.roll(v, wl - 1, 0)[off : off + wc]
    if c0 == 0:
        left = jnp.where(row_id == 0, 0.0, left)
    if c1 == W:
        right = jnp.where(row_id == wc - 1, 0.0, right)
    dst[rows, 0:C] = left.astype(BF16)
    dst[rows, C : 2 * C] = v[off : off + wc].astype(BF16)
    dst[rows, 2 * C : 3 * C] = right.astype(BF16)


def gate_into(mixed, gated, at, total, gain):
    one = total.astype(BF16)
    half = rms(one.astype(F32), gain * 0.5)
    mixed[at] = one
    gated[at] = (half + half * jnp.tanh(half)).astype(BF16)


def first_rows_kernel(info, latents, outer, inner, info_out):
    pass_on(info, info_out)
    k = info[0]
    outer[...] = latents[MAIN:8, 1 - k]
    inner[...] = latents[MAIN:8, k]


def first_rows_stage(info, latents):
    shape = jax.ShapeDtypeStruct((EDGE, W, C), BF16)
    return pl.pallas_call(
        first_rows_kernel,
        out_shape=(shape, shape, INFO),
        in_specs=[SMEM, VMEM],
        out_specs=(VMEM, VMEM, SMEM),
        compiler_params=pltpu.CompilerParams(vmem_limit_bytes=8 * 2**20),
        cost_estimate=LIGHT,
        name="first_rows",
    )(info, latents)


def other_rows_kernel(info, latents, w, *refs):
    *pieces, wv, info_out, sems = refs
    pass_on(info, info_out)
    k = info[0]
    copies = [
        pltpu.make_async_copy(w.at[tap], wv.at[role], sems.at[role])
        for role, tap in enumerate((1, 2 - 2 * k, 2 * k))
    ]
    for copy in copies:
        copy.start()
    for j in range(len(pieces) // 2):
        p0, p1 = piece_bounds(j)
        pieces[2 * j][...] = latents[0:MAIN, 1 - k, p0:p1, :]
        pieces[2 * j + 1][...] = latents[0:MAIN, k, p0:p1, :]
    for copy in copies:
        copy.wait()


def other_rows_stage(info, latents, w):
    shapes = []
    for j in range(len(CUTS) - 1):
        p0, p1 = piece_bounds(j)
        shapes += [jax.ShapeDtypeStruct((MAIN, p1 - p0, C), BF16)] * 2
    shapes.append(jax.ShapeDtypeStruct((3, 3 * C, C), BF16))
    return pl.pallas_call(
        other_rows_kernel,
        out_shape=shapes + [INFO],
        in_specs=[SMEM, VMEM, HBM],
        out_specs=[VMEM] * len(shapes) + [SMEM],
        scratch_shapes=[pltpu.SemaphoreType.DMA((3,))],
        compiler_params=pltpu.CompilerParams(vmem_limit_bytes=16 * 2**20),
        cost_estimate=LIGHT,
        name="other_rows",
    )(info, latents, w)


def edge_kernel(info, own, sib, same, cross, g1, g2, wv, mixed, gated, info_out, x):
    k = info[0]
    pass_on(info, info_out)
    gain = g1[...]
    gain_halo = gain * info[2].astype(F32)
    bounds = (0, W, 0, W)
    for slot in range(2):
        for role in range(3):
            for i in range(EDGE):
                if role < 2:
                    v = (own, sib)[slot][MAIN + i, k if role == 0 else 1 - k]
                else:
                    v = (same, cross)[slot][i]
                v = rms(v.astype(F32), gain_halo if role == 2 else gain)
                shifted_into(x.at[slot, role], slice(i * W, (i + 1) * W), v, bounds)
    for slot in range(2):
        total = (own, sib)[slot][MAIN:8, k].astype(F32).reshape(EDGE * W, C)
        for role in range(3):
            total = total + mm(x[slot, role], wv[role])
        at = pl.ds(EDGE * (k if slot == 0 else 1 - k), EDGE)
        gate_into(mixed, gated, at, total.reshape(EDGE, W, C), g2[...])


def edge_stage(info, own, sib, same, cross, g1, g2, w):
    shape = jax.ShapeDtypeStruct((2 * EDGE, W, C), BF16)
    return pl.pallas_call(
        edge_kernel,
        out_shape=(shape, shape, INFO),
        in_specs=[SMEM] + [VMEM] * 7,
        out_specs=(VMEM, VMEM, SMEM),
        scratch_shapes=[pltpu.VMEM((2, 3, EDGE * W, 3 * C), BF16)],
        compiler_params=pltpu.CompilerParams(vmem_limit_bytes=24 * 2**20),
        cost_estimate=LIGHT,
        name="edge",
    )(info, own, sib, same, cross, g1, g2, w)


def inner_kernel(j, info, own, sib, g1, wv, partial, info_out, x):
    pass_on(info, info_out)
    bounds = window(j)
    c0, c1, lo, hi = bounds
    wc = c1 - c0
    k = info[0]
    gain = g1[...]
    step = frames_per_step(MAIN, wc, 500)

    def prepare(index, role):
        for i in range(step):
            slot, at = divmod(index * step + i, MAIN)
            v = (own, sib)[slot][at, k if role == 0 else 1 - k, lo:hi, :].astype(F32)
            shifted_into(x.at[index % 2, role], slice(i * wc, (i + 1) * wc), rms(v, gain), bounds)

    for role in range(2):
        prepare(0, role)
    for index in range(2 * MAIN // step):
        slot, at = divmod(index * step, MAIN)
        acc = (own, sib)[slot][at : at + step, k, c0:c1, :].astype(F32).reshape(step * wc, C)
        for role in range(2):
            acc = acc + mm(x[index % 2, role], wv[role])
            if index + 1 < 2 * MAIN // step:
                prepare(index + 1, role)
        partial[index * step : (index + 1) * step] = acc.reshape(step, wc, C)


def inner_stage(j, info, own, sib, g1, wv):
    c0, c1, _, _ = window(j)
    wc = c1 - c0
    return pl.pallas_call(
        functools.partial(inner_kernel, j),
        out_shape=(jax.ShapeDtypeStruct((2 * MAIN, wc, C), F32), INFO),
        in_specs=[SMEM, VMEM, VMEM, VMEM, VMEM],
        out_specs=(VMEM, SMEM),
        scratch_shapes=[pltpu.VMEM((2, 2, frames_per_step(MAIN, wc, 500) * wc, 3 * C), BF16)],
        compiler_params=pltpu.CompilerParams(vmem_limit_bytes=20 * 2**20),
        cost_estimate=LIGHT,
        name=f"inner_{j}",
    )(info, own, sib, g1, wv)


def halo_kernel(j, n_pieces, info, partial, *refs):
    same = refs[:n_pieces]
    cross = refs[n_pieces : 2 * n_pieces]
    g1, g2, wv, mixed, gated, info_out, x = refs[2 * n_pieces :]
    pass_on(info, info_out)
    bounds = window(j)
    c0, c1, lo, hi = bounds
    wc = c1 - c0
    k = info[0]
    first = j + 1 - n_pieces
    gain_one = g1[...] * info[2].astype(F32)
    gain_two = g2[...]
    step = frames_per_step(MAIN, wc, 500)

    def prepare(index):
        for i in range(step):
            slot, at = divmod(index * step + i, MAIN)
            found = []
            for n in range(n_pieces):
                p0, p1 = piece_bounds(first + n)
                begin, end = max(p0, lo), min(p1, hi)
                found.append((same, cross)[slot][n][at, begin - p0 : end - p0, :].astype(F32))
            v = found[0] if n_pieces == 1 else jnp.concatenate(found, axis=0)
            shifted_into(x.at[index % 2], slice(i * wc, (i + 1) * wc), rms(v, gain_one), bounds)

    def finish(index, total):
        slot, at = divmod(index * step, MAIN)
        to = pl.ds(at + MAIN * (k if slot == 0 else 1 - k), step)
        gate_into(mixed, gated, to, total.reshape(step, wc, C), gain_two)

    prepare(0)
    last = None
    for index in range(2 * MAIN // step):
        total = partial[index * step : (index + 1) * step].reshape(step * wc, C)
        total = total + mm(x[index % 2], wv[2])
        if last is not None:
            finish(index - 1, last)
        if index + 1 < 2 * MAIN // step:
            prepare(index + 1)
        last = total
    finish(2 * MAIN // step - 1, last)


def halo_stage(j, info, partial, same, cross, g1, g2, wv):
    c0, c1, _, _ = window(j)
    wc = c1 - c0
    first = max(0, j - 1)
    same, cross = same[first : j + 1], cross[first : j + 1]
    n = len(same)
    shape = jax.ShapeDtypeStruct((2 * MAIN, wc, C), BF16)
    return pl.pallas_call(
        functools.partial(halo_kernel, j, n),
        out_shape=(shape, shape, INFO),
        in_specs=[SMEM] + [VMEM] * (2 * n + 4),
        out_specs=(VMEM, VMEM, SMEM),
        scratch_shapes=[pltpu.VMEM((2, frames_per_step(MAIN, wc, 500) * wc, 3 * C), BF16)],
        compiler_params=pltpu.CompilerParams(vmem_limit_bytes=18 * 2**20),
        cost_estimate=LIGHT,
        name=f"halo_{j}",
    )(info, partial, *same, *cross, g1, g2, wv)


def split_columns(j):
    wc = CUTS[j + 1] - CUTS[j]
    ring = RING if j == len(CUTS) - 2 else 0
    return (wc - ring, ring) if ring else (wc,)


def frames_into(x, wc, arrays):
    for f in range(NF - 1):
        at = (f + 1) * wc
        for array in arrays:
            x[at : at + array.shape[1]] = array[f]
            at += array.shape[1]


def place_of(f):
    core, at = divmod(f, 8)
    return (1, core * EDGE + at - MAIN) if at >= MAIN else (0, core * MAIN + at)


def temporal_kernel(j, info, gated, edge_gated, before, mixed, edge_mixed, w, g3, *refs):
    mixed_two, n_first, *n_rest, info_out, x = refs
    pass_on(info, info_out)
    c0, c1 = CUTS[j], CUTS[j + 1]
    wc = c1 - c0
    seen = before[:, c0:c1, :].reshape(2 * wc, C)
    x[0 : 2 * wc] = jnp.where(info[1] > 0, seen, jnp.zeros_like(seen))

    def frame(main, edge, f):
        which, at = place_of(f)
        return edge[at, c0:c1, :] if which else main[at]

    for f in range(NF):
        x[(f + 2) * wc : (f + 3) * wc] = frame(gated, edge_gated, f)
    gain = g3[...]
    step = frames_per_step(NF, wc, 320)
    for f0 in range(0, NF, step):
        acc = sum(
            mm(x[(f0 + tap) * wc : (f0 + tap + step) * wc, :], w[tap]) for tap in range(3)
        )
        for i in range(step):
            f = f0 + i
            base = frame(mixed, edge_mixed, f).astype(F32)
            two = (acc[i * wc : (i + 1) * wc] + base).astype(BF16)
            mixed_two[f] = two
            normed = rms(two.astype(F32), gain).astype(BF16)
            if f == 0:
                n_first[0] = normed
            else:
                at = 0
                for part in n_rest:
                    part[f - 1] = normed[at : at + part.shape[1]]
                    at += part.shape[1]


def temporal_stage(j, info, gated, edge_gated, before, mixed, edge_mixed, w, g3):
    wc = CUTS[j + 1] - CUTS[j]
    return pl.pallas_call(
        functools.partial(temporal_kernel, j),
        out_shape=(
            jax.ShapeDtypeStruct((NF, wc, C), BF16),
            jax.ShapeDtypeStruct((1, wc, C), BF16),
            *(jax.ShapeDtypeStruct((NF - 1, n, C), BF16) for n in split_columns(j)),
            INFO,
        ),
        in_specs=[SMEM] + [VMEM] * 7,
        out_specs=(VMEM,) * (2 + len(split_columns(j))) + (SMEM,),
        scratch_shapes=[pltpu.VMEM(((NF + 2) * wc, C), BF16)],
        compiler_params=pltpu.CompilerParams(vmem_limit_bytes=16 * 2**20),
        cost_estimate=LIGHT,
        name=f"temporal_{j}",
    )(info, gated, edge_gated, before, mixed, edge_mixed, w, g3)


def grouped_store(dst, frame, product, wc):
    for g in range(wc // 8):
        pair = jnp.concatenate(
            [product[g * 8 : g * 8 + 8], product[wc + g * 8 : wc + g * 8 + 8]], axis=0
        )
        dst[g, frame * 8 : frame * 8 + 16, :] = pair.astype(BF16)


def qkv_kernel(wc, count, info, n_first, *refs):
    n_rest, (wq, wk, wv, q, k, v, info_out, x) = refs[:count], refs[count:]
    pass_on(info, info_out)
    x[0:wc] = n_first[0]
    frames_into(x, wc, n_rest)
    for f0 in range(0, NF, 4):
        rows = x[f0 * wc : (f0 + 4) * wc, :]
        for w, dst, scale in ((wq, q, 0.125), (wk, k, None), (wv, v, None)):
            product = mm(rows, w[...])
            if scale is not None:
                product = product * scale
            grouped_store(dst, f0, product[: 2 * wc], wc)
            grouped_store(dst, f0 + 2, product[2 * wc :], wc)


def qkv_stage(j, info, n_first, n_rest, wq, wk, wv):
    wc = CUTS[j + 1] - CUTS[j]
    shape = jax.ShapeDtypeStruct((wc // 8, NF * 8, C), BF16)
    return pl.pallas_call(
        functools.partial(qkv_kernel, wc, len(n_rest)),
        out_shape=(shape, shape, shape, INFO),
        in_specs=[SMEM] + [VMEM] * (4 + len(n_rest)),
        out_specs=(VMEM, VMEM, VMEM, SMEM),
        scratch_shapes=[pltpu.VMEM((NF * wc, C), BF16)],
        compiler_params=pltpu.CompilerParams(vmem_limit_bytes=20 * 2**20),
        cost_estimate=LIGHT,
        name=f"project_{j}",
    )(info, n_first, *n_rest, wq, wk, wv)


def attend_kernel(wc, count, info, *refs):
    ctx, refs = refs[:count], refs[count:]
    wk, wv, wo, q, k, v, mixed_two, *blocks, info_out, x, kc, vc, att, out = refs
    pass_on(info, info_out)
    groups = wc // 8
    rows = NF * 8
    x[0:wc] = jnp.zeros((wc, C), BF16)
    frames_into(x, wc, ctx)
    for f0 in range(0, NF, 4):
        part = x[f0 * wc : (f0 + 4) * wc, :]
        for w, dst in ((wk, kc), (wv, vc)):
            product = mm(part, w[...])
            grouped_store(dst, f0, product[: 2 * wc], wc)
            grouped_store(dst, f0 + 2, product[2 * wc :], wc)
    row = lax.broadcasted_iota(jnp.int32, (rows, 2 * rows), 0)
    key = lax.broadcasted_iota(jnp.int32, (rows, 2 * rows), 1)
    lag = row // 8 + NF - key // 8
    allowed = (row % 8 == key % 8) & (lag >= 0) & (lag < NF)
    allowed = allowed & ((key >= rows) | (info[1] > 0))
    bias = jnp.where(allowed, 0.0, -1e30).astype(F32)
    lane_head = lax.broadcasted_iota(jnp.int32, (rows, 4 * HD), 1) // HD
    for g in range(groups):
        for half in range(2):
            lanes = slice(half * 4 * HD, (half + 1) * 4 * HD)
            keys = jnp.concatenate([kc[g, :, lanes], k[g, :, lanes]], axis=0)
            values = jnp.concatenate([vc[g, :, lanes], v[g, :, lanes]], axis=0)
            queries = q[g, :, lanes]
            stacked = jnp.concatenate(
                [jnp.where(lane_head == h, queries, jnp.zeros_like(queries)) for h in range(4)],
                axis=0,
            )
            score = lax.dot_general(
                stacked, keys, (((1,), (1,)), ((), ())), preferred_element_type=F32
            )
            score = score.reshape(4, rows, 2 * rows) + bias[None]
            e = jnp.exp(score - jnp.max(score, axis=-1, keepdims=True))
            scales = 1.0 / jnp.sum(e, axis=-1, keepdims=True)
            got = mm(e.astype(BF16).reshape(4 * rows, 2 * rows), values)
            total, scale = got[:rows], jnp.broadcast_to(scales[0], (rows, 4 * HD))
            for h in range(1, 4):
                total = jnp.where(lane_head == h, got[h * rows : (h + 1) * rows], total)
                scale = jnp.where(lane_head == h, scales[h], scale)
            total = total * scale
            att[g, :, lanes] = total.astype(BF16)
    for g in range(0, groups, 2):
        pair = att[g : g + 2].reshape(2 * rows, C)
        product = mm(pair, wo[...])
        for f in range(NF):
            piece = jnp.concatenate(
                [product[f * 8 : f * 8 + 8], product[rows + f * 8 : rows + f * 8 + 8]], axis=0
            )
            cols = slice(g * 8, g * 8 + 16)
            out[f, cols, :] = (piece + mixed_two[f, cols, :].astype(F32)).astype(BF16)
    core, band = info[0], info[3]
    for n in range(4):
        at = 2 * lax.rem(band + n, 4)
        blocks[n][0] = out[pl.ds(8 * core + at, 2)]
        blocks[n][1] = out[pl.ds(8 - 8 * core + at, 2)]


def attend_stage(j, info, ctx, wk, wv, wo, q, k, v, mixed_two):
    wc = CUTS[j + 1] - CUTS[j]
    groups = wc // 8
    return pl.pallas_call(
        functools.partial(attend_kernel, wc, len(ctx)),
        out_shape=(jax.ShapeDtypeStruct((2, 2, wc, C), BF16),) * 4 + (INFO,),
        in_specs=[SMEM] + [VMEM] * (7 + len(ctx)),
        out_specs=(VMEM,) * 4 + (SMEM,),
        scratch_shapes=[
            pltpu.VMEM((NF * wc, C), BF16),
            pltpu.VMEM((groups, NF * 8, C), BF16),
            pltpu.VMEM((groups, NF * 8, C), BF16),
            pltpu.VMEM((groups, NF * 8, C), BF16),
            pltpu.VMEM((NF, wc, C), BF16),
        ],
        compiler_params=pltpu.CompilerParams(vmem_limit_bytes=20 * 2**20),
        cost_estimate=LIGHT,
        name=f"attend_{j}",
    )(info, *ctx, wk, wv, wo, q, k, v, mixed_two)


def deal_kernel(info, *refs):
    blocks, (give, info_out) = refs[:4], refs[4:]
    pass_on(info, info_out)
    for n in range(4):
        give[n] = blocks[n][1]


def deal_stage(j, info, blocks):
    wc = CUTS[j + 1] - CUTS[j]
    return pl.pallas_call(
        deal_kernel,
        out_shape=(jax.ShapeDtypeStruct((4, 2, wc, C), BF16), INFO),
        in_specs=[SMEM] + [VMEM] * 4,
        out_specs=(VMEM, SMEM),
        compiler_params=pltpu.CompilerParams(vmem_limit_bytes=8 * 2**20),
        cost_estimate=LIGHT,
        name=f"deal_{j}",
    )(info, *blocks)


def place_kernel(j, info, *refs):
    blocks, got, (out, info_out, sems) = refs[:4], refs[4], refs[-3:]
    pass_on(info, info_out)
    c0, c1 = CUTS[j], CUTS[j + 1]
    core, band = info[0], info[3]
    copies = []
    for n in range(4):
        row = 2 * lax.rem(band + 4 - n, 4)
        for i, (src, at) in enumerate(((blocks[n].at[0], core), (got.at[n], 1 - core))):
            dst = out.at[:, row + at, c0:c1, :]
            copies.append(pltpu.make_async_copy(src, dst, sems.at[2 * n + i]))
    for copy in copies:
        copy.start()
    for copy in copies:
        copy.wait()


def place_stage(j, info, blocks, got, whole):
    earlier = () if whole is None else (whole,)
    return pl.pallas_call(
        functools.partial(place_kernel, j),
        out_shape=(jax.ShapeDtypeStruct((2, 8, W, C), BF16), INFO),
        in_specs=[SMEM] + [VMEM] * 5 + [HBM] * len(earlier),
        out_specs=(HBM, SMEM),
        scratch_shapes=[pltpu.SemaphoreType.DMA((8,))],
        input_output_aliases={6: 0} if earlier else {},
        compiler_params=pltpu.CompilerParams(vmem_limit_bytes=8 * 2**20),
        cost_estimate=LIGHT,
        name=f"place_{j}",
    )(info, *blocks, got, *earlier)


def shards(
    latents,
    gain_one,
    spatial_weight,
    gain_two,
    temporal_weight,
    gain_three,
    query_weight,
    key_weight,
    value_weight,
    out_weight,
):
    index = lax.axis_index("frames")
    row = lax.axis_index("rows")
    k = index % 2
    halo_is_inside = jnp.where(k == 0, row > 0, row < lax.axis_size("rows") - 1)
    info = jnp.stack([k, index // 2, halo_is_inside.astype(jnp.int32), row]).astype(jnp.int32)
    g1, g2, g3 = (g.reshape(1, C) for g in (gain_one, gain_two, gain_three))
    w1 = spatial_weight.reshape(3, 3 * C, C)
    parts = range(len(CUTS) - 1)

    sib = routed(latents, to_sibling)
    outer, inner, info = first_rows_stage(info, latents)
    edge_same, edge_cross = routed(outer, to_same_core), routed(inner, to_other_core)
    *pieces, weights, info = other_rows_stage(info, latents, w1)
    *pieces, edge_same, edge_cross = lax.optimization_barrier((*pieces, edge_same, edge_cross))
    own = latents
    same = [routed(piece, to_same_core) for piece in pieces[0::2]]
    cross = [routed(piece, to_other_core) for piece in pieces[1::2]]

    state = [{} for _ in parts]
    shared = {}

    def edge(j, info):
        shared["mixed"], shared["gated"], info = edge_stage(
            info, own, sib, edge_same, edge_cross, g1, g2, weights
        )
        shared["before"] = routed(shared["gated"][EDGE:], to_next_chip)
        return info

    def inside(j, info):
        state[j]["partial"], info = inner_stage(j, info, own, sib, g1, weights)
        return info

    def spatial(j, info):
        s = state[j]
        s["mixed"], s["gated"], info = halo_stage(
            j, info, s["partial"], same, cross, g1, g2, weights
        )
        return info

    def temporal(j, info):
        s = state[j]
        s["mixed"], s["first"], *s["rest"], info = temporal_stage(
            j,
            info,
            s["gated"],
            shared["gated"],
            shared["before"],
            s["mixed"],
            shared["mixed"],
            temporal_weight,
            g3,
        )
        s["ctx"] = [routed(s["rest"][0], to_next_chip)]
        if len(s["rest"]) > 1:
            s["ctx"].append(routed(s["rest"][1], to_chip_before))
        return info

    def project(j, info):
        s = state[j]
        s["q"], s["k"], s["v"], info = qkv_stage(
            j, info, s["first"], s["rest"], query_weight, key_weight, value_weight
        )
        if len(s["ctx"]) > 1:
            hop, s["q"] = lax.optimization_barrier((s["ctx"][1], s["q"]))
            s["ctx"][1] = routed(hop, to_chip_before)
        return info

    def attend(j, info):
        s = state[j]
        *blocks, info = attend_stage(
            j,
            info,
            s["ctx"],
            key_weight,
            value_weight,
            out_weight,
            s["q"],
            s["k"],
            s["v"],
            s["mixed"],
        )
        ring = state[-1]["ctx"]
        if j + 2 == len(state) and len(ring) > 1:
            hop, blocks[0] = lax.optimization_barrier((ring[1], blocks[0]))
            ring[1] = routed(hop, to_chip_before_last)
        for n in (2, 1, 3):
            blocks[n] = routed(blocks[n], lambda f, r: (f, r + n))
        s["blocks"] = blocks
        return info

    def deal(j, info):
        s = state[j]
        give, info = deal_stage(j, info, s["blocks"])
        if j + 1 < len(state):
            later = state[j + 1]["blocks"]
            give, *later[1:] = lax.optimization_barrier((give, *later[1:]))
        s["got"] = routed(give, to_sibling)
        return info

    def place(j, info):
        s = state[j]
        shared["out"], info = place_stage(j, info, s["blocks"], s["got"], shared.get("out"))
        return info

    stages = {
        "e": edge,
        "i": inside,
        "s": spatial,
        "t": temporal,
        "p": project,
        "a": attend,
        "d": deal,
        "w": place,
    }
    for step in ORDER:
        info = stages[step[0]](int(step[1]), info)
    return shared["out"].reshape(-1, C)


def solution(mesh):
    placed = (P("frames", "rows", None, None),) + (P(),) * 9
    return jax.shard_map(
        shards, mesh=mesh, in_specs=placed, out_specs=P(("frames", "rows"), None), check_vma=False
    )
```

```python
import functools

import jax
import jax.numpy as jnp
from jax import lax
from jax.experimental import pallas as pl
from jax.experimental.pallas import tpu as pltpu
from jax.sharding import PartitionSpec as P

C = 512
HEADS = 8
HD = 64
W = 128
NF = 16
RIM = 8
EDGE = 2
MAIN = 8 - EDGE
CUTS = (0, 64, 128)
RING = 16
ORDER = ("e0", "i0", "s0", "t0", "i1", "s1", "t1", "p0", "p1", "a0", "a1", "d0", "d1", "w0")
AXES = ("frames", "rows")
F32 = jnp.float32
BF16 = jnp.bfloat16
LIGHT = pl.CostEstimate(flops=0, bytes_accessed=0, transcendentals=0)
HBM = pl.BlockSpec(memory_space=pltpu.HBM)
SMEM = pl.BlockSpec(memory_space=pltpu.SMEM)
VMEM = pl.BlockSpec(memory_space=pltpu.VMEM)


def routed(x, route):
    frames, rows = lax.axis_size("frames"), lax.axis_size("rows")
    pairs = []
    for f in range(frames):
        for r in range(rows):
            to_f, to_r = route(f, r)
            pairs.append((f * rows + r, to_f % frames * rows + to_r % rows))
    return lax.ppermute(x, AXES, pairs)


def to_sibling(f, r):
    return f ^ 1, r


def to_same_core(f, r):
    return f, (r + 1 if f % 2 == 0 else r - 1)


def to_other_core(f, r):
    return f ^ 1, (r + 1 if f % 2 == 1 else r - 1)


def to_next_chip(f, r):
    return f + 2, r


def pass_on(info, info_out):
    for i in range(4):
        info_out[i] = info[i]


INFO = jax.ShapeDtypeStruct((4,), jnp.int32)


def to_chip_before(f, r):
    core, x = f % 2, f // 2 % 4
    return f // 8 * 8 + (x - 1) % 4 * 2 + core, r


def to_chip_before_last(f, r):
    to_f, _ = to_chip_before(f, r)
    return (to_f + 8 if f // 2 % 4 == 1 else to_f), r


def rms(v, gain):
    mean_square = jnp.mean(v * v, axis=-1, keepdims=True)
    return v * lax.rsqrt(mean_square + 1e-06) * gain


def mm(a, b):
    return jnp.dot(a, b, preferred_element_type=F32)


def piece_bounds(j):
    lo = 0 if j == 0 else CUTS[j] + RIM
    hi = W if j == len(CUTS) - 2 else CUTS[j + 1] + RIM
    return lo, hi


def frames_per_step(count, wc, rows):
    step = max(1, rows // wc)
    while count % step:
        step -= 1
    return step


def window(j):
    c0, c1 = CUTS[j], CUTS[j + 1]
    return c0, c1, max(c0 - 8, 0), min(c1 + 8, W)


def shifted_into(dst, rows, v, bounds):
    c0, c1, lo, hi = bounds
    wc, wl, off = c1 - c0, hi - lo, c0 - lo
    row_id = lax.broadcasted_iota(jnp.int32, (wc, C), 0)
    left = pltpu.roll(v, 1, 0)[off : off + wc]
    right = pltpu.roll(v, wl - 1, 0)[off : off + wc]
    if c0 == 0:
        left = jnp.where(row_id == 0, 0.0, left)
    if c1 == W:
        right = jnp.where(row_id == wc - 1, 0.0, right)
    dst[rows, 0:C] = left.astype(BF16)
    dst[rows, C : 2 * C] = v[off : off + wc].astype(BF16)
    dst[rows, 2 * C : 3 * C] = right.astype(BF16)


def gate_into(mixed, gated, at, total, gain):
    one = total.astype(BF16)
    half = rms(one.astype(F32), gain * 0.5)
    mixed[at] = one
    gated[at] = (half + half * jnp.tanh(half)).astype(BF16)


def first_rows_kernel(info, latents, outer, inner, info_out):
    pass_on(info, info_out)
    k = info[0]
    outer[...] = latents[MAIN:8, 1 - k]
    inner[...] = latents[MAIN:8, k]


def first_rows_stage(info, latents):
    shape = jax.ShapeDtypeStruct((EDGE, W, C), BF16)
    return pl.pallas_call(
        first_rows_kernel,
        out_shape=(shape, shape, INFO),
        in_specs=[SMEM, VMEM],
        out_specs=(VMEM, VMEM, SMEM),
        compiler_params=pltpu.CompilerParams(vmem_limit_bytes=8 * 2**20),
        cost_estimate=LIGHT,
        name="first_rows",
    )(info, latents)


def other_rows_kernel(info, latents, w, *refs):
    *pieces, wv, info_out, sems = refs
    pass_on(info, info_out)
    k = info[0]
    copies = [
        pltpu.make_async_copy(w.at[tap], wv.at[role], sems.at[role])
        for role, tap in enumerate((1, 2 - 2 * k, 2 * k))
    ]
    for copy in copies:
        copy.start()
    for j in range(len(pieces) // 2):
        p0, p1 = piece_bounds(j)
        pieces[2 * j][...] = latents[0:MAIN, 1 - k, p0:p1, :]
        pieces[2 * j + 1][...] = latents[0:MAIN, k, p0:p1, :]
    for copy in copies:
        copy.wait()


def other_rows_stage(info, latents, w):
    shapes = []
    for j in range(len(CUTS) - 1):
        p0, p1 = piece_bounds(j)
        shapes += [jax.ShapeDtypeStruct((MAIN, p1 - p0, C), BF16)] * 2
    shapes.append(jax.ShapeDtypeStruct((3, 3 * C, C), BF16))
    return pl.pallas_call(
        other_rows_kernel,
        out_shape=shapes + [INFO],
        in_specs=[SMEM, VMEM, HBM],
        out_specs=[VMEM] * len(shapes) + [SMEM],
        scratch_shapes=[pltpu.SemaphoreType.DMA((3,))],
        compiler_params=pltpu.CompilerParams(vmem_limit_bytes=16 * 2**20),
        cost_estimate=LIGHT,
        name="other_rows",
    )(info, latents, w)


def edge_kernel(info, own, sib, same, cross, g1, g2, wv, mixed, gated, info_out, x):
    k = info[0]
    pass_on(info, info_out)
    gain = g1[...]
    gain_halo = gain * info[2].astype(F32)
    bounds = (0, W, 0, W)
    for slot in range(2):
        for role in range(3):
            for i in range(EDGE):
                if role < 2:
                    v = (own, sib)[slot][MAIN + i, k if role == 0 else 1 - k]
                else:
                    v = (same, cross)[slot][i]
                v = rms(v.astype(F32), gain_halo if role == 2 else gain)
                shifted_into(x.at[slot, role], slice(i * W, (i + 1) * W), v, bounds)
    for slot in range(2):
        total = (own, sib)[slot][MAIN:8, k].astype(F32).reshape(EDGE * W, C)
        for role in range(3):
            total = total + mm(x[slot, role], wv[role])
        at = pl.ds(EDGE * (k if slot == 0 else 1 - k), EDGE)
        gate_into(mixed, gated, at, total.reshape(EDGE, W, C), g2[...])


def edge_stage(info, own, sib, same, cross, g1, g2, w):
    shape = jax.ShapeDtypeStruct((2 * EDGE, W, C), BF16)
    return pl.pallas_call(
        edge_kernel,
        out_shape=(shape, shape, INFO),
        in_specs=[SMEM] + [VMEM] * 7,
        out_specs=(VMEM, VMEM, SMEM),
        scratch_shapes=[pltpu.VMEM((2, 3, EDGE * W, 3 * C), BF16)],
        compiler_params=pltpu.CompilerParams(vmem_limit_bytes=24 * 2**20),
        cost_estimate=LIGHT,
        name="edge",
    )(info, own, sib, same, cross, g1, g2, w)


def inner_kernel(j, info, own, sib, g1, wv, partial, info_out, x):
    pass_on(info, info_out)
    bounds = window(j)
    c0, c1, lo, hi = bounds
    wc = c1 - c0
    k = info[0]
    gain = g1[...]
    step = frames_per_step(MAIN, wc, 500)

    def prepare(index, role):
        for i in range(step):
            slot, at = divmod(index * step + i, MAIN)
            v = (own, sib)[slot][at, k if role == 0 else 1 - k, lo:hi, :].astype(F32)
            shifted_into(x.at[index % 2, role], slice(i * wc, (i + 1) * wc), rms(v, gain), bounds)

    for role in range(2):
        prepare(0, role)
    for index in range(2 * MAIN // step):
        slot, at = divmod(index * step, MAIN)
        acc = (own, sib)[slot][at : at + step, k, c0:c1, :].astype(F32).reshape(step * wc, C)
        for role in range(2):
            acc = acc + mm(x[index % 2, role], wv[role])
            if index + 1 < 2 * MAIN // step:
                prepare(index + 1, role)
        partial[index * step : (index + 1) * step] = acc.reshape(step, wc, C)


def inner_stage(j, info, own, sib, g1, wv):
    c0, c1, _, _ = window(j)
    wc = c1 - c0
    return pl.pallas_call(
        functools.partial(inner_kernel, j),
        out_shape=(jax.ShapeDtypeStruct((2 * MAIN, wc, C), F32), INFO),
        in_specs=[SMEM, VMEM, VMEM, VMEM, VMEM],
        out_specs=(VMEM, SMEM),
        scratch_shapes=[pltpu.VMEM((2, 2, frames_per_step(MAIN, wc, 500) * wc, 3 * C), BF16)],
        compiler_params=pltpu.CompilerParams(vmem_limit_bytes=20 * 2**20),
        cost_estimate=LIGHT,
        name=f"inner_{j}",
    )(info, own, sib, g1, wv)


def halo_kernel(j, n_pieces, info, partial, *refs):
    same = refs[:n_pieces]
    cross = refs[n_pieces : 2 * n_pieces]
    g1, g2, wv, mixed, gated, info_out, x = refs[2 * n_pieces :]
    pass_on(info, info_out)
    bounds = window(j)
    c0, c1, lo, hi = bounds
    wc = c1 - c0
    k = info[0]
    first = j + 1 - n_pieces
    gain_one = g1[...] * info[2].astype(F32)
    gain_two = g2[...]
    step = frames_per_step(MAIN, wc, 500)

    def prepare(index):
        for i in range(step):
            slot, at = divmod(index * step + i, MAIN)
            found = []
            for n in range(n_pieces):
                p0, p1 = piece_bounds(first + n)
                begin, end = max(p0, lo), min(p1, hi)
                found.append((same, cross)[slot][n][at, begin - p0 : end - p0, :].astype(F32))
            v = found[0] if n_pieces == 1 else jnp.concatenate(found, axis=0)
            shifted_into(x.at[index % 2], slice(i * wc, (i + 1) * wc), rms(v, gain_one), bounds)

    def finish(index, total):
        slot, at = divmod(index * step, MAIN)
        to = pl.ds(at + MAIN * (k if slot == 0 else 1 - k), step)
        gate_into(mixed, gated, to, total.reshape(step, wc, C), gain_two)

    prepare(0)
    last = None
    for index in range(2 * MAIN // step):
        total = partial[index * step : (index + 1) * step].reshape(step * wc, C)
        total = total + mm(x[index % 2], wv[2])
        if last is not None:
            finish(index - 1, last)
        if index + 1 < 2 * MAIN // step:
            prepare(index + 1)
        last = total
    finish(2 * MAIN // step - 1, last)


def halo_stage(j, info, partial, same, cross, g1, g2, wv):
    c0, c1, _, _ = window(j)
    wc = c1 - c0
    first = max(0, j - 1)
    same, cross = same[first : j + 1], cross[first : j + 1]
    n = len(same)
    shape = jax.ShapeDtypeStruct((2 * MAIN, wc, C), BF16)
    return pl.pallas_call(
        functools.partial(halo_kernel, j, n),
        out_shape=(shape, shape, INFO),
        in_specs=[SMEM] + [VMEM] * (2 * n + 4),
        out_specs=(VMEM, VMEM, SMEM),
        scratch_shapes=[pltpu.VMEM((2, frames_per_step(MAIN, wc, 500) * wc, 3 * C), BF16)],
        compiler_params=pltpu.CompilerParams(vmem_limit_bytes=18 * 2**20),
        cost_estimate=LIGHT,
        name=f"halo_{j}",
    )(info, partial, *same, *cross, g1, g2, wv)


def split_columns(j):
    wc = CUTS[j + 1] - CUTS[j]
    ring = RING if j == len(CUTS) - 2 else 0
    return (wc - ring, ring) if ring else (wc,)


def frames_into(x, wc, arrays):
    for f in range(NF - 1):
        at = (f + 1) * wc
        for array in arrays:
            x[at : at + array.shape[1]] = array[f]
            at += array.shape[1]


def place_of(f):
    core, at = divmod(f, 8)
    return (1, core * EDGE + at - MAIN) if at >= MAIN else (0, core * MAIN + at)


def temporal_kernel(j, info, gated, edge_gated, before, mixed, edge_mixed, w, g3, *refs):
    mixed_two, n_first, *n_rest, info_out, x = refs
    pass_on(info, info_out)
    c0, c1 = CUTS[j], CUTS[j + 1]
    wc = c1 - c0
    seen = before[:, c0:c1, :].reshape(2 * wc, C)
    x[0 : 2 * wc] = jnp.where(info[1] > 0, seen, jnp.zeros_like(seen))

    def frame(main, edge, f):
        which, at = place_of(f)
        return edge[at, c0:c1, :] if which else main[at]

    for f in range(NF):
        x[(f + 2) * wc : (f + 3) * wc] = frame(gated, edge_gated, f)
    gain = g3[...]
    step = frames_per_step(NF, wc, 320)
    for f0 in range(0, NF, step):
        acc = sum(
            mm(x[(f0 + tap) * wc : (f0 + tap + step) * wc, :], w[tap]) for tap in range(3)
        )
        for i in range(step):
            f = f0 + i
            base = frame(mixed, edge_mixed, f).astype(F32)
            two = (acc[i * wc : (i + 1) * wc] + base).astype(BF16)
            mixed_two[f] = two
            normed = rms(two.astype(F32), gain).astype(BF16)
            if f == 0:
                n_first[0] = normed
            else:
                at = 0
                for part in n_rest:
                    part[f - 1] = normed[at : at + part.shape[1]]
                    at += part.shape[1]


def temporal_stage(j, info, gated, edge_gated, before, mixed, edge_mixed, w, g3):
    wc = CUTS[j + 1] - CUTS[j]
    return pl.pallas_call(
        functools.partial(temporal_kernel, j),
        out_shape=(
            jax.ShapeDtypeStruct((NF, wc, C), BF16),
            jax.ShapeDtypeStruct((1, wc, C), BF16),
            *(jax.ShapeDtypeStruct((NF - 1, n, C), BF16) for n in split_columns(j)),
            INFO,
        ),
        in_specs=[SMEM] + [VMEM] * 7,
        out_specs=(VMEM,) * (2 + len(split_columns(j))) + (SMEM,),
        scratch_shapes=[pltpu.VMEM(((NF + 2) * wc, C), BF16)],
        compiler_params=pltpu.CompilerParams(vmem_limit_bytes=16 * 2**20),
        cost_estimate=LIGHT,
        name=f"temporal_{j}",
    )(info, gated, edge_gated, before, mixed, edge_mixed, w, g3)


def grouped_store(dst, frame, product, wc):
    for g in range(wc // 8):
        pair = jnp.concatenate(
            [product[g * 8 : g * 8 + 8], product[wc + g * 8 : wc + g * 8 + 8]], axis=0
        )
        dst[g, frame * 8 : frame * 8 + 16, :] = pair.astype(BF16)


def qkv_kernel(wc, count, info, n_first, *refs):
    n_rest, (wq, wk, wv, q, k, v, info_out, x) = refs[:count], refs[count:]
    pass_on(info, info_out)
    x[0:wc] = n_first[0]
    frames_into(x, wc, n_rest)
    for f0 in range(0, NF, 4):
        rows = x[f0 * wc : (f0 + 4) * wc, :]
        for w, dst, scale in ((wq, q, 0.125), (wk, k, None), (wv, v, None)):
            product = mm(rows, w[...])
            if scale is not None:
                product = product * scale
            grouped_store(dst, f0, product[: 2 * wc], wc)
            grouped_store(dst, f0 + 2, product[2 * wc :], wc)


def qkv_stage(j, info, n_first, n_rest, wq, wk, wv):
    wc = CUTS[j + 1] - CUTS[j]
    shape = jax.ShapeDtypeStruct((wc // 8, NF * 8, C), BF16)
    return pl.pallas_call(
        functools.partial(qkv_kernel, wc, len(n_rest)),
        out_shape=(shape, shape, shape, INFO),
        in_specs=[SMEM] + [VMEM] * (4 + len(n_rest)),
        out_specs=(VMEM, VMEM, VMEM, SMEM),
        scratch_shapes=[pltpu.VMEM((NF * wc, C), BF16)],
        compiler_params=pltpu.CompilerParams(vmem_limit_bytes=20 * 2**20),
        cost_estimate=LIGHT,
        name=f"project_{j}",
    )(info, n_first, *n_rest, wq, wk, wv)


def attend_kernel(wc, count, info, *refs):
    ctx, refs = refs[:count], refs[count:]
    wk, wv, wo, q, k, v, mixed_two, *blocks, info_out, x, kc, vc, att, out = refs
    pass_on(info, info_out)
    groups = wc // 8
    rows = NF * 8
    x[0:wc] = jnp.zeros((wc, C), BF16)
    frames_into(x, wc, ctx)
    for f0 in range(0, NF, 4):
        part = x[f0 * wc : (f0 + 4) * wc, :]
        for w, dst in ((wk, kc), (wv, vc)):
            product = mm(part, w[...])
            grouped_store(dst, f0, product[: 2 * wc], wc)
            grouped_store(dst, f0 + 2, product[2 * wc :], wc)
    row = lax.broadcasted_iota(jnp.int32, (rows, 2 * rows), 0)
    key = lax.broadcasted_iota(jnp.int32, (rows, 2 * rows), 1)
    lag = row // 8 + NF - key // 8
    allowed = (row % 8 == key % 8) & (lag >= 0) & (lag < NF)
    allowed = allowed & ((key >= rows) | (info[1] > 0))
    bias = jnp.where(allowed, 0.0, -1e30).astype(F32)
    lane_head = lax.broadcasted_iota(jnp.int32, (rows, 4 * HD), 1) // HD
    for g in range(groups):
        for half in range(2):
            lanes = slice(half * 4 * HD, (half + 1) * 4 * HD)
            keys = jnp.concatenate([kc[g, :, lanes], k[g, :, lanes]], axis=0)
            values = jnp.concatenate([vc[g, :, lanes], v[g, :, lanes]], axis=0)
            queries = q[g, :, lanes]
            stacked = jnp.concatenate(
                [jnp.where(lane_head == h, queries, jnp.zeros_like(queries)) for h in range(4)],
                axis=0,
            )
            score = lax.dot_general(
                stacked, keys, (((1,), (1,)), ((), ())), preferred_element_type=F32
            )
            score = score.reshape(4, rows, 2 * rows) + bias[None]
            e = jnp.exp(score - jnp.max(score, axis=-1, keepdims=True))
            scales = 1.0 / jnp.sum(e, axis=-1, keepdims=True)
            got = mm(e.astype(BF16).reshape(4 * rows, 2 * rows), values)
            total, scale = got[:rows], jnp.broadcast_to(scales[0], (rows, 4 * HD))
            for h in range(1, 4):
                total = jnp.where(lane_head == h, got[h * rows : (h + 1) * rows], total)
                scale = jnp.where(lane_head == h, scales[h], scale)
            total = total * scale
            att[g, :, lanes] = total.astype(BF16)
    for g in range(0, groups, 2):
        pair = att[g : g + 2].reshape(2 * rows, C)
        product = mm(pair, wo[...])
        for f in range(NF):
            piece = jnp.concatenate(
                [product[f * 8 : f * 8 + 8], product[rows + f * 8 : rows + f * 8 + 8]], axis=0
            )
            cols = slice(g * 8, g * 8 + 16)
            out[f, cols, :] = (piece + mixed_two[f, cols, :].astype(F32)).astype(BF16)
    core, band = info[0], info[3]
    for n in range(4):
        at = 2 * lax.rem(band + n, 4)
        blocks[n][0] = out[pl.ds(8 * core + at, 2)]
        blocks[n][1] = out[pl.ds(8 - 8 * core + at, 2)]


def attend_stage(j, info, ctx, wk, wv, wo, q, k, v, mixed_two):
    wc = CUTS[j + 1] - CUTS[j]
    groups = wc // 8
    return pl.pallas_call(
        functools.partial(attend_kernel, wc, len(ctx)),
        out_shape=(jax.ShapeDtypeStruct((2, 2, wc, C), BF16),) * 4 + (INFO,),
        in_specs=[SMEM] + [VMEM] * (7 + len(ctx)),
        out_specs=(VMEM,) * 4 + (SMEM,),
        scratch_shapes=[
            pltpu.VMEM((NF * wc, C), BF16),
            pltpu.VMEM((groups, NF * 8, C), BF16),
            pltpu.VMEM((groups, NF * 8, C), BF16),
            pltpu.VMEM((groups, NF * 8, C), BF16),
            pltpu.VMEM((NF, wc, C), BF16),
        ],
        compiler_params=pltpu.CompilerParams(vmem_limit_bytes=20 * 2**20),
        cost_estimate=LIGHT,
        name=f"attend_{j}",
    )(info, *ctx, wk, wv, wo, q, k, v, mixed_two)


def deal_kernel(info, *refs):
    blocks, (give, info_out) = refs[:4], refs[4:]
    pass_on(info, info_out)
    for n in range(4):
        give[n] = blocks[n][1]


def deal_stage(j, info, blocks):
    wc = CUTS[j + 1] - CUTS[j]
    return pl.pallas_call(
        deal_kernel,
        out_shape=(jax.ShapeDtypeStruct((4, 2, wc, C), BF16), INFO),
        in_specs=[SMEM] + [VMEM] * 4,
        out_specs=(VMEM, SMEM),
        compiler_params=pltpu.CompilerParams(vmem_limit_bytes=8 * 2**20),
        cost_estimate=LIGHT,
        name=f"deal_{j}",
    )(info, *blocks)


def place_kernel(info, *refs):
    blocks, (out, info_out, sems) = refs[:-3], refs[-3:]
    pass_on(info, info_out)
    core, band = info[0], info[3]
    copies = []
    for j in range(len(CUTS) - 1):
        c0, c1 = CUTS[j], CUTS[j + 1]
        *kept, got = blocks[5 * j : 5 * j + 5]
        for n in range(4):
            row = 2 * lax.rem(band + 4 - n, 4)
            for src, at in ((kept[n].at[0], core), (got.at[n], 1 - core)):
                dst = out.at[:, row + at, c0:c1, :]
                copies.append(pltpu.make_async_copy(src, dst, sems.at[len(copies)]))
    for copy in copies:
        copy.start()
    for copy in copies:
        copy.wait()


def place_stage(info, blocks):
    return pl.pallas_call(
        place_kernel,
        out_shape=(jax.ShapeDtypeStruct((2, 8, W, C), BF16), INFO),
        in_specs=[SMEM] + [VMEM] * len(blocks),
        out_specs=(HBM, SMEM),
        scratch_shapes=[pltpu.SemaphoreType.DMA((8 * (len(CUTS) - 1),))],
        compiler_params=pltpu.CompilerParams(vmem_limit_bytes=8 * 2**20),
        cost_estimate=LIGHT,
        name="place",
    )(info, *blocks)


def shards(
    latents,
    gain_one,
    spatial_weight,
    gain_two,
    temporal_weight,
    gain_three,
    query_weight,
    key_weight,
    value_weight,
    out_weight,
):
    index = lax.axis_index("frames")
    row = lax.axis_index("rows")
    k = index % 2
    halo_is_inside = jnp.where(k == 0, row > 0, row < lax.axis_size("rows") - 1)
    info = jnp.stack([k, index // 2, halo_is_inside.astype(jnp.int32), row]).astype(jnp.int32)
    g1, g2, g3 = (g.reshape(1, C) for g in (gain_one, gain_two, gain_three))
    w1 = spatial_weight.reshape(3, 3 * C, C)
    parts = range(len(CUTS) - 1)

    sib = routed(latents, to_sibling)
    outer, inner, info = first_rows_stage(info, latents)
    edge_same, edge_cross = routed(outer, to_same_core), routed(inner, to_other_core)
    *pieces, weights, info = other_rows_stage(info, latents, w1)
    *pieces, edge_same, edge_cross = lax.optimization_barrier((*pieces, edge_same, edge_cross))
    own = latents
    same = [routed(piece, to_same_core) for piece in pieces[0::2]]
    cross = [routed(piece, to_other_core) for piece in pieces[1::2]]

    state = [{} for _ in parts]
    shared = {}

    def edge(j, info):
        shared["mixed"], shared["gated"], info = edge_stage(
            info, own, sib, edge_same, edge_cross, g1, g2, weights
        )
        shared["before"] = routed(shared["gated"][EDGE:], to_next_chip)
        return info

    def inside(j, info):
        state[j]["partial"], info = inner_stage(j, info, own, sib, g1, weights)
        return info

    def spatial(j, info):
        s = state[j]
        s["mixed"], s["gated"], info = halo_stage(
            j, info, s["partial"], same, cross, g1, g2, weights
        )
        return info

    def temporal(j, info):
        s = state[j]
        s["mixed"], s["first"], *s["rest"], info = temporal_stage(
            j,
            info,
            s["gated"],
            shared["gated"],
            shared["before"],
            s["mixed"],
            shared["mixed"],
            temporal_weight,
            g3,
        )
        s["ctx"] = [routed(s["rest"][0], to_next_chip)]
        if len(s["rest"]) > 1:
            s["ctx"].append(routed(s["rest"][1], to_chip_before))
        return info

    def project(j, info):
        s = state[j]
        s["q"], s["k"], s["v"], info = qkv_stage(
            j, info, s["first"], s["rest"], query_weight, key_weight, value_weight
        )
        if len(s["ctx"]) > 1:
            hop, s["q"] = lax.optimization_barrier((s["ctx"][1], s["q"]))
            s["ctx"][1] = routed(hop, to_chip_before)
        return info

    def attend(j, info):
        s = state[j]
        *blocks, info = attend_stage(
            j,
            info,
            s["ctx"],
            key_weight,
            value_weight,
            out_weight,
            s["q"],
            s["k"],
            s["v"],
            s["mixed"],
        )
        ring = state[-1]["ctx"]
        if j + 2 == len(state) and len(ring) > 1:
            hop, blocks[0] = lax.optimization_barrier((ring[1], blocks[0]))
            ring[1] = routed(hop, to_chip_before_last)
        for n in (2, 1, 3):
            blocks[n] = routed(blocks[n], lambda f, r: (f, r + n))
        s["blocks"] = blocks
        return info

    def deal(j, info):
        s = state[j]
        give, info = deal_stage(j, info, s["blocks"])
        if j + 1 < len(state):
            later = state[j + 1]["blocks"]
            give, *later[1:] = lax.optimization_barrier((give, *later[1:]))
        s["got"] = routed(give, to_sibling)
        return info

    def place(j, info):
        blocks = [block for s in state for block in (*s["blocks"], s["got"])]
        shared["out"], info = place_stage(info, blocks)
        return info

    stages = {
        "e": edge,
        "i": inside,
        "s": spatial,
        "t": temporal,
        "p": project,
        "a": attend,
        "d": deal,
        "w": place,
    }
    for step in ORDER:
        info = stages[step[0]](int(step[1]), info)
    return shared["out"].reshape(-1, C)


def solution(mesh):
    placed = (P("frames", "rows", None, None),) + (P(),) * 9
    return jax.shard_map(
        shards, mesh=mesh, in_specs=placed, out_specs=P(("frames", "rows"), None), check_vma=False
    )
```
